32 devices in a mesh: row: 8 (over y, x, core), col: 4 (over z).
Axes of the slice: x: 2, y: 2, z: 4, core: 2. Of those that a mesh axis runs over, the one named last changes fastest.
Arguments:
- kernel: float32 [5120, 5120], P('row', 'col'), as said below
Outputs:
- factored: float32 [5120, 5120], P('row', 'col')
Inputs may be any that keep to these rules, and one draw needn't show every extreme that they name: `kernel`: in global order symmetric positive definite; its eigenvalues are at least 0.05.
All inputs are finite; a program needn't handle non-finite values.
Results may differ from the reference program's by a relative error of at most 0.0003.
Values sent between devices are 32-bit elements; how exact they have to be, the bound alone decides.
A program may use at most 128 MiB of HBM per device.

```python
import jax
import jax.numpy as jnp
from jax import lax

NB = 128
FEATURES = 512
N = 5120
N_ROW = 8
N_COL = 4


def element_order(blocks_dev, groups):
    place = jnp.arange(N // NB, dtype=jnp.int32)
    glob = place % blocks_dev * groups + place // blocks_dev
    return (glob[:, None] * NB + jnp.arange(NB, dtype=jnp.int32)[None, :]).reshape(-1)


def draw_kernel(key, part):
    key = jax.random.fold_in(key, 7)
    feat_key, diag_key = jax.random.split(key)
    features = jax.random.randint(feat_key, (N, FEATURES), -4, 5).astype(jnp.float32)
    extra = jnp.exp(jax.random.uniform(diag_key, (N,), jnp.float32, jnp.log(0.05), jnp.log(0.5)))
    row_el = element_order(N // (NB * N_ROW), N_ROW)
    col_el = element_order(N // (NB * N_COL), N_COL)
    row_pos = jnp.argsort(row_el, stable=True).astype(jnp.int32)
    col_pos = jnp.argsort(col_el, stable=True).astype(jnp.int32)
    gram = jnp.dot(features[row_el], features[col_el].T, precision=lax.Precision.HIGHEST) * jnp.float32(1.0 / 4096.0)
    return gram.at[row_pos, col_pos].add(extra)


def setup_inputs(seed: int = 0) -> dict:
    key_list = jax.random.split(jax.random.key(seed), 2)
    kernel = draw_kernel(jax.random.fold_in(key_list[1], 71), 0)
    return dict(kernel=kernel)


def row_global(count, blocks):
    place = jnp.arange(count, dtype=jnp.int32)
    return place % blocks * N_ROW + place // blocks

def col_global(count, blocks):
    place = jnp.arange(count, dtype=jnp.int32)
    return place % blocks * N_COL + place // blocks

def reference(kernel):
    order = kernel.shape[0]
    blocks_r = order // (NB * N_ROW)
    blocks_c = order // (NB * N_COL)
    rows_g = row_global(order // NB, blocks_r)
    cols_g = col_global(order // NB, blocks_c)
    matrix = kernel
    panels = []
    for step in range(2):
        place_r = step % N_ROW * blocks_r + step // N_ROW
        place_c = step % N_COL * blocks_c + step // N_COL
        corner = matrix[place_r * NB:(place_r + 1) * NB, place_c * NB:(place_c + 1) * NB]
        lower = jnp.linalg.cholesky(corner)
        inverse = lax.linalg.triangular_solve(lower, jnp.eye(NB, dtype=lower.dtype), left_side=True, lower=True)
        column = matrix[:, place_c * NB:(place_c + 1) * NB]
        solved = jnp.dot(column, inverse.T, precision=lax.Precision.HIGHEST).reshape(order // NB, NB, NB)
        panel = jnp.where((rows_g < step)[:, None, None], jnp.float32(0.0), jnp.where((rows_g == step)[:, None, None], lower[None], solved))
        glob = panel.reshape(N_ROW, blocks_r, NB, NB).transpose(1, 0, 2, 3).reshape(order // NB, NB, NB)
        by_cols = glob.reshape(blocks_c, N_COL, NB, NB).transpose(1, 0, 2, 3).reshape(order, NB)
        panel = panel.reshape(order, NB)
        matrix = matrix - jnp.dot(panel, by_cols.T, precision=lax.Precision.HIGHEST)
        panels.append((place_c, panel))
    row_mask = jnp.repeat(rows_g < 2, NB)
    col_mask = jnp.repeat(cols_g >= 2, NB)
    result = jnp.where(row_mask[:, None] & col_mask[None, :], jnp.float32(0.0), matrix)
    for place_c, panel in panels:
        result = lax.dynamic_update_slice(result, panel, (0, place_c * NB))
    return result
```

```python
import functools
import math

import jax
import jax.numpy as jnp
from jax import lax
from jax.experimental import pallas as pl
from jax.experimental.pallas import tpu as pltpu
from jax.sharding import PartitionSpec as P

NB = 128
SUB = 8
CW = 256
TILE = 256
MESH = pl.DeviceIdType.MESH
f32 = jnp.float32
bf16 = jnp.bfloat16


def dot(a, b, ca=1, cb=0):
    return lax.dot_general(
        a,
        b,
        (((ca,), (cb,)), ((), ())),
        precision=lax.Precision.HIGHEST,
        preferred_element_type=f32,
    )


def split(x):
    h = x.astype(bf16).astype(f32)
    rest = x - h
    m = rest.astype(bf16).astype(f32)
    return h, m, rest - m


def eliminate(aug, steps):
    row = lax.broadcasted_iota(jnp.int32, (SUB, 2 * NB), 0)
    for b in range(NB // SUB):
        lo = b * SUB
        block = aug[lo : lo + SUB, :]
        rows = [jnp.broadcast_to(block[k : k + 1, :], (SUB, 2 * NB)) for k in range(SUB)]
        d = {}
        for k in range(SUB):
            for j in range(k, SUB):
                d[k, j] = jnp.broadcast_to(rows[k][:, lo + j : lo + j + 1], (SUB, NB))
        for j in range(SUB):
            inv = lax.rsqrt(d[j, j])
            rows[j] = rows[j] * jnp.concatenate([inv, inv], axis=1)
            for i in range(j + 1, SUB):
                d[j, i] = d[j, i] * inv
            for i in range(j + 1, SUB):
                m = d[j, i]
                for l in range(i, SUB):
                    d[i, l] = d[i, l] - m * d[j, l]
                rows[i] = rows[i] - jnp.concatenate([m, m], axis=1) * rows[j]
        u = rows[0]
        for k in range(1, SUB):
            u = jnp.where(row == k, rows[k], u)
        aug[lo : lo + SUB, :] = u
        if lo + SUB < NB:
            h, m, l = split(u)
            left = jnp.concatenate([h, h, m, h, m, l], axis=0)[:, :NB].T[lo + SUB :, :]
            right = jnp.concatenate([h, m, h, l, m, h], axis=0)
            aug[lo + SUB :, :] = aug[lo + SUB :, :] - jnp.dot(
                left.astype(bf16), right.astype(bf16), preferred_element_type=f32
            )
        for step in steps.pop(0) if steps else ():
            step()


def panels_kernel(
    nrow, ncol, rows_here, cols_here,
    a, r_out, c_out,
    p, ac, k, aug, low, fac,
    psend, precv, zsend, ksend, ksib, krecv, asend, arecv, loc,
):
    chips = nrow // 2
    nx = math.isqrt(chips)
    ny = chips // nx
    nt = rows_here // NB
    na = cols_here // CW
    r = lax.axis_index("row")
    c = lax.axis_index("col")
    core = lax.rem(r, 2)
    q = r // 2
    qx = lax.rem(q, nx)
    qy = q // nx
    sib = r + 1 - 2 * core
    first = core == 0

    barrier = pltpu.get_barrier_semaphore()
    for i in range(1, ncol):
        pl.semaphore_signal(barrier, inc=1, device_id=(r, lax.rem(c + i, ncol)), device_id_type=MESH)
    for i in range(1, chips):
        pl.semaphore_signal(
            barrier, inc=1, device_id=(lax.rem(q + i, chips) * 2 + core, c), device_id_type=MESH
        )
    pl.semaphore_signal(barrier, inc=1, device_id=(sib, c), device_id_type=MESH)
    pl.semaphore_wait(barrier, ncol - 1 + chips)

    started = []

    def send(cond, src, dst, ss, rs, dev):
        def make():
            return pltpu.make_async_remote_copy(
                src_ref=src, dst_ref=dst, send_sem=ss, recv_sem=rs, device_id=dev, device_id_type=MESH
            )

        @pl.when(cond)
        def _():
            make().start()

        started.append((cond, make))

    def received(cond, dst, rs):
        @pl.when(cond)
        def _():
            pltpu.make_async_remote_copy(
                src_ref=dst, dst_ref=dst, send_sem=loc.at[3], recv_sem=rs,
                device_id=(sib, c), device_id_type=MESH,
            ).wait_recv()

    def pc(s, t):
        return p.at[s, pl.ds(t * NB, NB)]

    def ach(s, t):
        return ac.at[s, :, pl.ds(t * CW, CW)]

    def a_rows(t):
        return a.at[pl.ds(t * NB, NB), pl.ds(0, NB)]

    def own(i):
        if i == 0:
            return c == 0, pltpu.make_async_copy(a.at[:, pl.ds(0, NB)], p.at[0], loc.at[0])
        if i == 1:
            return c == 1, pltpu.make_async_copy(a.at[:, pl.ds(0, NB)], p.at[1], loc.at[1])
        return None

    for z in range(ncol - 1, 0, -1):
        send((r == 0) & (c == 0), a_rows(0), pc(0, 0), zsend.at[z], precv.at[0, 0], (r, z))

    def spread(s, cond, src):
        base = 0 if s == 0 else 1
        for j in range(chips - 1, 0, -1):
            send(cond, src, k.at[s], ksend.at[s, j], krecv.at[s], (2 * j + base, c))
        send(cond, src, k.at[s], ksib.at[s], krecv.at[s], (sib, c))

    for i in range(2):
        cond, copy = own(i)
        pl.when(cond)(copy.start)
    for s in range(2):
        @pl.when(r == s)
        def _():
            pltpu.make_async_copy(a.at[pl.ds(0, NB), :], ac.at[s], loc.at[2]).start()

    def p_source(t):
        first_sent = (c == 0) & (r != 0) if t == 0 else c == 0
        send(first_sent, a_rows(t), pc(0, t), psend.at[0, t, 0], precv.at[0, t], (r, 1))
        send(c == 1, a_rows(t), pc(1, t), psend.at[1, t, 0], precv.at[1, t], (r, 0))
        if ncol > 2:
            send(c == 1, a_rows(t), pc(1, t), psend.at[1, t, 1], precv.at[1, t], (r, 2))

    p_source(0)
    received((r == 0) & (c != 0), pc(0, 0), precv.at[0, 0])
    for i in range(2):
        cond, copy = own(i)
        pl.when(cond)(copy.wait)
    spread(0, r == 0, pc(0, 0))

    def a_children(cond, s, t, src, base):
        down = (qy < ny - 1) if s else (qy < ny - 1) & (qx == 0)
        over = (qx < nx - 1) & (qy == 0) if s else (qx < nx - 1)
        send(cond & over, src, ach(s, t), asend.at[s, t, 0], arecv.at[s, t], (r + 2, c))
        send(cond & down, src, ach(s, t), asend.at[s, t, 1], arecv.at[s, t], (r + 2 * nx, c))
        send(cond, src, ach(s, t), asend.at[s, t, 2], arecv.at[s, t], (sib, c))

    def a_source(t):
        for s in range(2):
            a_children(r == s, s, t, a.at[pl.ds(0, NB), pl.ds(t * CW, CW)], s)

    for t in range(1, nt):
        p_source(t)
    for t in range(na):
        a_source(t)

    received((q != 0) & first, k.at[0], krecv.at[0])
    send((q != 0) & first, k.at[0], k.at[0], ksib.at[0], krecv.at[0], (sib, c))
    received(core == 1, k.at[0], krecv.at[0])

    def p_pass(t):
        if t == 0:
            received((c != 0) & (r != 0), pc(0, 0), precv.at[0, 0])
            received(c != 1, pc(1, 0), precv.at[1, 0])
        else:
            received((c > 0) & (c < ncol - 1), pc(0, t), precv.at[0, t])
            received((c > 1) & (c < ncol - 1), pc(1, t), precv.at[1, t])
        go = (c > 0) & (c < ncol - 1)
        send(go & (r != 0) if t == 0 else go, pc(0, t), pc(0, t), psend.at[0, t, 0], precv.at[0, t], (r, c + 1))
        send((c > 1) & (c < ncol - 1), pc(1, t), pc(1, t), psend.at[1, t, 0], precv.at[1, t], (r, c + 1))

    def k_first():
        spread(1, r == 1, pc(0, 0))
        spread(2, r == 1, pc(1, 0))

    def k_pass():
        for s in (1, 2):
            cond = (core == 1) & (q != 0)
            received(cond, k.at[s], krecv.at[s])
            send(cond, k.at[s], k.at[s], ksib.at[s], krecv.at[s], (sib, c))

    def a_pass(t):
        for s in range(2):
            cond = (q != 0) & (core == s)
            received(cond, ach(s, t), arecv.at[s, t])
            a_children(cond, s, t, ach(s, t), s)

    items = [functools.partial(p_pass, 0), k_first, functools.partial(a_pass, 0), k_pass]
    for t in range(1, max(nt, na)):
        if t < nt:
            items.append(functools.partial(p_pass, t))
        if t < na:
            items.append(functools.partial(a_pass, t))
    half = NB // SUB
    places = [[] for _ in range(2 * half)]
    for n, item in enumerate(items):
        places[min(1 + 2 * n, 2 * half - 1)].append(item)
    for n in range(4):
        if items[n] not in sum(places[:half], []):
            raise ValueError("order")

    eye = jnp.where(
        lax.broadcasted_iota(jnp.int32, (NB, NB), 0) == lax.broadcasted_iota(jnp.int32, (NB, NB), 1),
        f32(1.0), f32(0.0),
    )

    @pl.when(r == 0)
    def _():
        aug[0, :, :NB] = p[0, :NB, :]

    @pl.when(r != 0)
    def _():
        aug[0, :, :NB] = k[0]

    aug[0, :, NB:] = eye
    eliminate(aug.at[0], places[:half])

    received(first, k.at[1], krecv.at[1])
    received(first, k.at[2], krecv.at[2])

    @pl.when(r == 1)
    def _():
        k[1] = p[0, :NB, :]
        k[2] = p[1, :NB, :]

    w0 = aug[0, :, NB:]
    low[...] = dot(k[1], w0, 1, 1)
    l10 = low[...]
    aug[1, :, :NB] = k[2] - dot(l10, l10, 1, 1)
    aug[1, :, NB:] = eye
    eliminate(aug.at[1], places[half:])

    upper = lax.broadcasted_iota(jnp.int32, (NB, NB), 0) <= lax.broadcasted_iota(jnp.int32, (NB, NB), 1)
    fac[0] = jnp.where(upper, aug[0, :, :NB], f32(0.0)).T
    fac[1] = jnp.where(upper, aug[1, :, :NB], f32(0.0)).T

    for t in range(1, nt):
        received(c == ncol - 1, pc(0, t), precv.at[0, t])
        received((c == 0) | ((c == ncol - 1) & (c != 1)), pc(1, t), precv.at[1, t])
    for s in range(2):
        @pl.when(r == s)
        def _():
            pltpu.make_async_copy(a.at[pl.ds(0, NB), :], ac.at[s], loc.at[2]).wait()

    for t in range(nt):
        here = slice(t * NB, (t + 1) * NB)
        p0 = dot(p[0, here, :], aug[0, :, NB:], 1, 1)
        p1 = dot(p[1, here, :] - dot(p0, low[...], 1, 1), aug[1, :, NB:], 1, 1)
        r_out[here, :NB] = p0
        r_out[here, NB:] = p1

    @pl.when(r == 0)
    def _():
        r_out[:NB, :NB] = fac[0]
        r_out[:NB, NB:] = jnp.zeros((NB, NB), f32)

    @pl.when(r == 1)
    def _():
        r_out[:NB, NB:] = fac[1]

    for t in range(na):
        received(first, ach(1, t), arecv.at[1, t])
        received(core == 1, ach(0, t), arecv.at[0, t])
        here = slice(t * CW, (t + 1) * CW)
        c0 = dot(aug[0, :, NB:], ac[0, :, here])
        c1 = dot(aug[1, :, NB:], ac[1, :, here] - dot(low[...], c0))
        c_out[:NB, here] = c0
        c_out[NB:, here] = c1

    for cond, make in started:
        @pl.when(cond)
        def _():
            make().wait_send()


def update_kernel(a, left, right, out, parts):
    r = lax.axis_index("row")
    c = lax.axis_index("col")
    j = pl.program_id(0)

    @pl.when(j == 0)
    def _():
        x = left[...]
        h = x.astype(bf16)
        parts[0] = h
        parts[1] = (x - h.astype(f32)).astype(bf16)

    y = right[...]
    yh = y.astype(bf16)
    yl = (y - yh.astype(f32)).astype(bf16)
    mm = functools.partial(jnp.dot, preferred_element_type=f32)
    out[...] = a[...] - (mm(parts[0], yh) + (mm(parts[0], yl) + mm(parts[1], yh)))

    @pl.when(r < 2)
    def _():
        out[:NB, :] = jnp.zeros((NB, out.shape[1]), f32)

    for s in range(2):
        @pl.when((j == 0) & (c == s))
        def _():
            out[:, :NB] = left[:, s * NB : (s + 1) * NB]


def local(nrow, ncol, kernel):
    rows, cols = kernel.shape
    nt = rows // NB
    na = cols // CW
    chips = nrow // 2
    dma = pltpu.SemaphoreType.DMA
    left, right = pl.pallas_call(
        functools.partial(panels_kernel, nrow, ncol, rows, cols),
        out_shape=[
            jax.ShapeDtypeStruct((rows, 2 * NB), f32),
            jax.ShapeDtypeStruct((2 * NB, cols), f32),
        ],
        in_specs=[pl.BlockSpec(memory_space=pl.ANY)],
        out_specs=[pl.BlockSpec(memory_space=pltpu.VMEM)] * 2,
        scratch_shapes=[
            pltpu.VMEM((2, rows, NB), f32),
            pltpu.VMEM((2, NB, cols), f32),
            pltpu.VMEM((3, NB, NB), f32),
            pltpu.VMEM((2, NB, 2 * NB), f32),
            pltpu.VMEM((NB, NB), f32),
            pltpu.VMEM((2, NB, NB), f32),
            dma((2, nt, 2)),
            dma((2, nt)),
            dma((ncol,)),
            dma((3, chips)),
            dma((3,)),
            dma((3,)),
            dma((2, na, 3)),
            dma((2, na)),
            dma((4,)),
        ],
        compiler_params=pltpu.CompilerParams(
            collective_id=0, has_side_effects=True, vmem_limit_bytes=48 * 1024 * 1024
        ),
        name="panels",
    )(kernel)
    return pl.pallas_call(
        update_kernel,
        out_shape=jax.ShapeDtypeStruct((rows, cols), f32),
        grid=(cols // TILE,),
        in_specs=[
            pl.BlockSpec((rows, TILE), lambda j: (0, j)),
            pl.BlockSpec((rows, 2 * NB), lambda j: (0, 0)),
            pl.BlockSpec((2 * NB, TILE), lambda j: (0, j)),
        ],
        out_specs=pl.BlockSpec((rows, TILE), lambda j: (0, j)),
        scratch_shapes=[pltpu.VMEM((2, rows, 2 * NB), bf16)],
        compiler_params=pltpu.CompilerParams(vmem_limit_bytes=32 * 1024 * 1024),
        name="update",
    )(kernel, left, right)


def solution(mesh):
    return jax.shard_map(
        functools.partial(local, mesh.shape["row"], mesh.shape["col"]),
        mesh=mesh,
        in_specs=(P("row", "col"),),
        out_specs=P("row", "col"),
        check_vma=False,
    )
```

```python
import functools
import math

import jax
import jax.numpy as jnp
from jax import lax
from jax.experimental import pallas as pl
from jax.experimental.pallas import tpu as pltpu
from jax.sharding import PartitionSpec as P

NB = 128
SUB = 8
GROUP = 32
CW = 256
TILE = 256
MESH = pl.DeviceIdType.MESH
f32 = jnp.float32
bf16 = jnp.bfloat16


def dot(a, b, ca=1, cb=0):
    return lax.dot_general(
        a,
        b,
        (((ca,), (cb,)), ((), ())),
        precision=lax.Precision.HIGHEST,
        preferred_element_type=f32,
    )


def split(x):
    h = x.astype(bf16).astype(f32)
    rest = x - h
    m = rest.astype(bf16).astype(f32)
    return h, m, rest - m


def two(x):
    h = x.astype(bf16)
    return h, (x - h.astype(f32)).astype(bf16)


def mm(a, b):
    return jnp.dot(a, b, preferred_element_type=f32)


def splat(x, lane):
    return jnp.broadcast_to(x[:, lane : lane + 1], (SUB, NB))


def eliminate(aug, steps):
    row = lax.broadcasted_iota(jnp.int32, (SUB, NB), 0)
    subs = GROUP // SUB
    for g in range(NB // GROUP):
        top = g * GROUP
        rows = [
            [[jnp.broadcast_to(block[k : k + 1, h * NB : (h + 1) * NB], (SUB, NB)) for h in range(2)] for k in range(SUB)]
            for block in (aug[top + s * SUB : top + (s + 1) * SUB, :] for s in range(subs))
        ]
        done = []
        for s in range(subs):
            lo = top + s * SUB
            mine = rows[s]
            wide = 2 * SUB if s + 1 < subs else SUB
            d = {(k, j): splat(mine[k][0], lo + j) for k in range(SUB) for j in range(k, wide)}
            for j in range(SUB):
                inv = lax.rsqrt(d[j, j])
                for i in range(j + 1, wide):
                    d[j, i] = d[j, i] * inv
                for i in range(j + 1, SUB):
                    for l in range(i, wide):
                        d[i, l] = d[i, l] - d[j, i] * d[j, l]
                mine[j] = [x * inv for x in mine[j]]
                for i in range(j + 1, SUB):
                    mine[i] = [x - d[j, i] * y for x, y in zip(mine[i], mine[j])]
            for later in range(s + 1, subs):
                for i in range(SUB):
                    for k in range(SUB):
                        m = d[k, SUB + i] if later == s + 1 else splat(mine[k][0], top + later * SUB + i)
                        rows[later][i] = [x - m * y for x, y in zip(rows[later][i], mine[k])]
            halves = []
            for h in range(2):
                u = mine[0][h]
                for k in range(1, SUB):
                    u = jnp.where(row == k, mine[k][h], u)
                halves.append(u)
            done.append(jnp.concatenate(halves, axis=1))
        u = jnp.concatenate(done, axis=0)
        aug[top : top + GROUP, :] = u
        if top + GROUP < NB:
            h, m, l = split(u)
            left = jnp.concatenate([h, h, m, h, m, l], axis=0)[:, :NB].astype(bf16)
            right = jnp.concatenate([h, m, h, l, m, h], axis=0).astype(bf16)
            taken = lax.dot_general(left, right, (((0,), (0,)), ((), ())), preferred_element_type=f32)
            aug[top + GROUP :, :] = aug[top + GROUP :, :] - taken[top + GROUP :, :]
        for step in steps.pop(0) if steps else ():
            step()


def panels_kernel(
    nrow, ncol, rows_here, cols_here,
    a, panel, left, right,
    p, ac, k, aug, low,
    psend, precv, zsend, ksend, ksib, krecv, asend, arecv, loc,
):
    chips = nrow // 2
    nx = math.isqrt(chips)
    ny = chips // nx
    nt = rows_here // NB
    na = cols_here // CW
    r = lax.axis_index("row")
    c = lax.axis_index("col")
    core = lax.rem(r, 2)
    q = r // 2
    qx = lax.rem(q, nx)
    qy = q // nx
    sib = r + 1 - 2 * core
    first = core == 0

    barrier = pltpu.get_barrier_semaphore()
    for i in range(1, ncol):
        pl.semaphore_signal(barrier, inc=1, device_id=(r, lax.rem(c + i, ncol)), device_id_type=MESH)
    for i in range(1, chips):
        pl.semaphore_signal(
            barrier, inc=1, device_id=(lax.rem(q + i, chips) * 2 + core, c), device_id_type=MESH
        )
    pl.semaphore_signal(barrier, inc=1, device_id=(sib, c), device_id_type=MESH)
    pl.semaphore_wait(barrier, ncol - 1 + chips)

    started = []

    def send(cond, src, dst, ss, rs, dev):
        def make():
            return pltpu.make_async_remote_copy(
                src_ref=src, dst_ref=dst, send_sem=ss, recv_sem=rs, device_id=dev, device_id_type=MESH
            )

        @pl.when(cond)
        def _():
            make().start()

        started.append((cond, make))

    def received(cond, dst, rs):
        @pl.when(cond)
        def _():
            pltpu.make_async_remote_copy(
                src_ref=dst, dst_ref=dst, send_sem=loc.at[3], recv_sem=rs,
                device_id=(sib, c), device_id_type=MESH,
            ).wait_recv()

    def pc(s, t):
        return p.at[s, pl.ds(t * NB, NB)]

    def ach(s, t):
        return ac.at[s, :, pl.ds(t * CW, CW)]

    def a_rows(t):
        return a.at[pl.ds(t * NB, NB), pl.ds(0, NB)]

    def own(i):
        if i == 0:
            return c == 0, pltpu.make_async_copy(a.at[:, pl.ds(0, NB)], p.at[0], loc.at[0])
        if i == 1:
            return c == 1, pltpu.make_async_copy(a.at[:, pl.ds(0, NB)], p.at[1], loc.at[1])
        return None

    for z in range(ncol - 1, 0, -1):
        send((r == 0) & (c == 0), a_rows(0), pc(0, 0), zsend.at[z], precv.at[0, 0], (r, z))

    def spread(s, cond, src):
        base = 0 if s == 0 else 1
        for j in range(chips - 1, 0, -1):
            send(cond, src, k.at[s], ksend.at[s, j], krecv.at[s], (2 * j + base, c))
        send(cond, src, k.at[s], ksib.at[s], krecv.at[s], (sib, c))

    for i in range(2):
        cond, copy = own(i)
        pl.when(cond)(copy.start)
    for s in range(2):
        @pl.when(r == s)
        def _():
            pltpu.make_async_copy(a.at[pl.ds(0, NB), :], ac.at[s], loc.at[2]).start()

    def p_source(t, here):
        zero = here & (c == 0) & (r != 0) if t == 0 else here & (c == 0)
        one = here & (c == 1)
        send(zero, a_rows(t), pc(0, t), psend.at[0, t, 0], precv.at[0, t], (r, 1))
        send(one, a_rows(t), pc(1, t), psend.at[1, t, 0], precv.at[1, t], (r, 0))
        if ncol > 2:
            send(one, a_rows(t), pc(1, t), psend.at[1, t, 1], precv.at[1, t], (r, 2))

    received((r == 0) & (c != 0), pc(0, 0), precv.at[0, 0])
    for i in range(2):
        cond, copy = own(i)
        pl.when(cond)(copy.wait)
    spread(0, r == 0, pc(0, 0))

    def a_children(cond, s, t, src, base):
        down = (qy < ny - 1) if s else (qy < ny - 1) & (qx == 0)
        over = (qx < nx - 1) & (qy == 0) if s else (qx < nx - 1)
        send(cond & over, src, ach(s, t), asend.at[s, t, 0], arecv.at[s, t], (r + 2, c))
        send(cond & down, src, ach(s, t), asend.at[s, t, 1], arecv.at[s, t], (r + 2 * nx, c))
        send(cond, src, ach(s, t), asend.at[s, t, 2], arecv.at[s, t], (sib, c))

    def a_source(t):
        for s in range(2):
            a_children(r == s, s, t, a.at[pl.ds(0, NB), pl.ds(t * CW, CW)], s)

    for t in range(nt):
        p_source(t, q != 0)

    received((q != 0) & first, k.at[0], krecv.at[0])
    send((q != 0) & first, k.at[0], k.at[0], ksib.at[0], krecv.at[0], (sib, c))
    received(core == 1, k.at[0], krecv.at[0])

    def p_pass(t):
        if t == 0:
            received((c != 0) & (r != 0), pc(0, 0), precv.at[0, 0])
            received(c != 1, pc(1, 0), precv.at[1, 0])
        else:
            received((c > 0) & (c < ncol - 1), pc(0, t), precv.at[0, t])
            received((c > 1) & (c < ncol - 1), pc(1, t), precv.at[1, t])
        go = (c > 0) & (c < ncol - 1)
        send(go & (r != 0) if t == 0 else go, pc(0, t), pc(0, t), psend.at[0, t, 0], precv.at[0, t], (r, c + 1))
        send((c > 1) & (c < ncol - 1), pc(1, t), pc(1, t), psend.at[1, t, 0], precv.at[1, t], (r, c + 1))

    def k_first():
        spread(1, r == 1, pc(0, 0))
        spread(2, r == 1, pc(1, 0))

    def k_pass():
        for s in (1, 2):
            cond = (core == 1) & (q != 0)
            received(cond, k.at[s], krecv.at[s])
            send(cond, k.at[s], k.at[s], ksib.at[s], krecv.at[s], (sib, c))

    def a_pass(t):
        for s in range(2):
            cond = (q != 0) & (core == s)
            received(cond, ach(s, t), arecv.at[s, t])
            a_children(cond, s, t, ach(s, t), s)

    half = NB // GROUP
    places = [[] for _ in range(2 * half)]
    places[0] += [functools.partial(p_source, 0, q == 0)]
    places[0] += [functools.partial(p_pass, 0), k_first]
    places[0] += [functools.partial(p_source, t, q == 0) for t in range(1, nt)]
    places[1] += [functools.partial(a_source, t) for t in range(na)]
    places[2] += [k_pass]
    for t in range(max(nt, na)):
        at = places[min(3 + t, 2 * half - 1)]
        if 1 <= t < nt:
            at.append(functools.partial(p_pass, t))
        if t < na:
            at.append(functools.partial(a_pass, t))

    eye = jnp.where(
        lax.broadcasted_iota(jnp.int32, (NB, NB), 0) == lax.broadcasted_iota(jnp.int32, (NB, NB), 1),
        f32(1.0), f32(0.0),
    )

    @pl.when(r == 0)
    def _():
        aug[0, :, :NB] = p[0, :NB, :]

    @pl.when(r != 0)
    def _():
        aug[0, :, :NB] = k[0]

    aug[0, :, NB:] = eye
    eliminate(aug.at[0], places[:half])

    received(first, k.at[1], krecv.at[1])
    received(first, k.at[2], krecv.at[2])

    @pl.when(r == 1)
    def _():
        k[1] = p[0, :NB, :]
        k[2] = p[1, :NB, :]

    w0 = aug[0, :, NB:]
    low[...] = dot(k[1], w0, 1, 1)
    l10 = low[...]
    aug[1, :, :NB] = k[2] - dot(l10, l10, 1, 1)
    aug[1, :, NB:] = eye
    eliminate(aug.at[1], places[half:])

    w1 = aug[1, :, NB:]
    w10 = -dot(w1, dot(l10, w0))
    w = jnp.concatenate(
        [jnp.concatenate([w0, jnp.zeros((NB, NB), f32)], axis=1), jnp.concatenate([w10, w1], axis=1)], axis=0
    )
    wh, wl = two(w)
    w_left = jnp.concatenate([wh, wl, wh], axis=1)
    wh, wl = two(w.T)
    w_right = jnp.concatenate([wh, wh, wl], axis=0)

    for t in range(1, nt):
        received(c == ncol - 1, pc(0, t), precv.at[0, t])
        received((c == 0) | ((c == ncol - 1) & (c != 1)), pc(1, t), precv.at[1, t])
    for s in range(2):
        @pl.when(r == s)
        def _():
            pltpu.make_async_copy(a.at[pl.ds(0, NB), :], ac.at[s], loc.at[2]).wait()

    rh0, rl0 = two(p[0])
    rh1, rl1 = two(p[1])
    rows = mm(jnp.concatenate([rh0, rh1, rl0, rl1, rh0, rh1], axis=1), w_right)
    panel[...] = rows
    rh, rl = two(rows)
    left[...] = jnp.concatenate([rh, rl, rh], axis=1)

    upper = lax.broadcasted_iota(jnp.int32, (NB, NB), 0) <= lax.broadcasted_iota(jnp.int32, (NB, NB), 1)

    @pl.when(r == 0)
    def _():
        panel[:NB, :NB] = jnp.where(upper, aug[0, :, :NB], f32(0.0)).T
        panel[:NB, NB:] = jnp.zeros((NB, NB), f32)

    @pl.when(r == 1)
    def _():
        panel[:NB, NB:] = jnp.where(upper, aug[1, :, :NB], f32(0.0)).T

    for t in range(na):
        received(first, ach(1, t), arecv.at[1, t])
        received(core == 1, ach(0, t), arecv.at[0, t])
        here = slice(t * CW, (t + 1) * CW)
        h0, l0 = two(ac[0, :, here])
        h1, l1 = two(ac[1, :, here])
        cols = mm(w_left, jnp.concatenate([h0, h1, h0, h1, l0, l1], axis=0))
        ch, cl = two(cols)
        right[:, here] = jnp.concatenate([ch, ch, cl], axis=0)

    for cond, make in started:
        @pl.when(cond)
        def _():
            make().wait_send()


def update_kernel(a, panel, left, right, out, held, sems):
    r = lax.axis_index("row")
    c = lax.axis_index("col")
    copies = []
    for t in range(a.shape[1] // TILE):
        here = pl.ds(t * TILE, TILE)
        held[:, here] = a[:, here] - mm(left[...], right[:, here])

        @pl.when(r < 2)
        def _():
            held[:NB, here] = jnp.zeros((NB, TILE), f32)

        if t == 0:
            for s in range(2):
                @pl.when(c == s)
                def _():
                    held[:, :NB] = panel[:, s * NB : (s + 1) * NB]

        copy = pltpu.make_async_copy(held.at[:, here], out.at[:, here], sems.at[t])
        copy.start()
        copies.append(copy)
    for copy in copies:
        copy.wait()


def local(nrow, ncol, kernel):
    rows, cols = kernel.shape
    nt = rows // NB
    na = cols // CW
    chips = nrow // 2
    dma = pltpu.SemaphoreType.DMA
    panel, left, right = pl.pallas_call(
        functools.partial(panels_kernel, nrow, ncol, rows, cols),
        out_shape=[
            jax.ShapeDtypeStruct((rows, 2 * NB), f32),
            jax.ShapeDtypeStruct((rows, 6 * NB), bf16),
            jax.ShapeDtypeStruct((6 * NB, cols), bf16),
        ],
        in_specs=[pl.BlockSpec(memory_space=pltpu.HBM)],
        out_specs=[pl.BlockSpec(memory_space=pltpu.VMEM)] * 3,
        scratch_shapes=[
            pltpu.VMEM((2, rows, NB), f32),
            pltpu.VMEM((2, NB, cols), f32),
            pltpu.VMEM((3, NB, NB), f32),
            pltpu.VMEM((2, NB, 2 * NB), f32),
            pltpu.VMEM((NB, NB), f32),
            dma((2, nt, 2)),
            dma((2, nt)),
            dma((ncol,)),
            dma((3, chips)),
            dma((3,)),
            dma((3,)),
            dma((2, na, 3)),
            dma((2, na)),
            dma((4,)),
        ],
        compiler_params=pltpu.CompilerParams(
            collective_id=0, has_side_effects=True, vmem_limit_bytes=48 * 1024 * 1024
        ),
        name="panels",
    )(kernel)
    return pl.pallas_call(
        update_kernel,
        out_shape=jax.ShapeDtypeStruct((rows, cols), f32),
        in_specs=[pl.BlockSpec(memory_space=pltpu.VMEM)] * 4,
        out_specs=pl.BlockSpec(memory_space=pltpu.HBM),
        scratch_shapes=[pltpu.VMEM((rows, cols), f32), pltpu.SemaphoreType.DMA((cols // TILE,))],
        compiler_params=pltpu.CompilerParams(vmem_limit_bytes=32 * 1024 * 1024),
        name="update",
    )(kernel, panel, left, right)


def solution(mesh):
    return jax.shard_map(
        functools.partial(local, mesh.shape["row"], mesh.shape["col"]),
        mesh=mesh,
        in_specs=(P("row", "col"),),
        out_specs=P("row", "col"),
        check_vma=False,
    )
```

```python
import functools
import math

import jax
import jax.numpy as jnp
from jax import lax
from jax.experimental import pallas as pl
from jax.experimental.pallas import tpu as pltpu
from jax.sharding import PartitionSpec as P

NB = 128
SUB = 8
GROUP = 32
CW = 256
TILE = 256
MESH = pl.DeviceIdType.MESH
f32 = jnp.float32
bf16 = jnp.bfloat16


def dot(a, b, ca=1, cb=0):
    return lax.dot_general(
        a,
        b,
        (((ca,), (cb,)), ((), ())),
        precision=lax.Precision.HIGHEST,
        preferred_element_type=f32,
    )


def split(x):
    h = x.astype(bf16).astype(f32)
    rest = x - h
    m = rest.astype(bf16).astype(f32)
    return h, m, rest - m


def two(x):
    h = x.astype(bf16)
    return h, (x - h.astype(f32)).astype(bf16)


def mm(a, b):
    return jnp.dot(a, b, preferred_element_type=f32)


def splat(x, lane):
    return jnp.broadcast_to(x[:, lane : lane + 1], (SUB, NB))


def eliminate(aug, steps):
    row = lax.broadcasted_iota(jnp.int32, (SUB, NB), 0)
    subs = GROUP // SUB
    for g in range(NB // GROUP):
        top = g * GROUP
        rows = [
            [[jnp.broadcast_to(block[k : k + 1, h * NB : (h + 1) * NB], (SUB, NB)) for h in range(2)] for k in range(SUB)]
            for block in (aug[top + s * SUB : top + (s + 1) * SUB, :] for s in range(subs))
        ]
        done = []
        for s in range(subs):
            lo = top + s * SUB
            mine = rows[s]
            wide = 2 * SUB if s + 1 < subs else SUB
            d = {(k, j): splat(mine[k][0], lo + j) for k in range(SUB) for j in range(k, wide)}
            for j in range(SUB):
                inv = lax.rsqrt(d[j, j])
                for i in range(j + 1, wide):
                    d[j, i] = d[j, i] * inv
                for i in range(j + 1, SUB):
                    for l in range(i, wide):
                        d[i, l] = d[i, l] - d[j, i] * d[j, l]
                mine[j] = [x * inv for x in mine[j]]
                for i in range(j + 1, SUB):
                    mine[i] = [x - d[j, i] * y for x, y in zip(mine[i], mine[j])]
            for later in range(s + 1, subs):
                for i in range(SUB):
                    for k in range(SUB):
                        m = d[k, SUB + i] if later == s + 1 else splat(mine[k][0], top + later * SUB + i)
                        rows[later][i] = [x - m * y for x, y in zip(rows[later][i], mine[k])]
            halves = []
            for h in range(2):
                u = mine[0][h]
                for k in range(1, SUB):
                    u = jnp.where(row == k, mine[k][h], u)
                halves.append(u)
            done.append(jnp.concatenate(halves, axis=1))
            if s % 2 and s + 1 < subs:
                for step in steps.pop(0):
                    step()
        u = jnp.concatenate(done, axis=0)
        aug[top : top + GROUP, :] = u
        if top + GROUP < NB:
            h, m, l = split(u)
            left = jnp.concatenate([h, h, m, h, m, l], axis=0)[:, :NB].astype(bf16)
            right = jnp.concatenate([h, m, h, l, m, h], axis=0).astype(bf16)
            taken = lax.dot_general(left, right, (((0,), (0,)), ((), ())), preferred_element_type=f32)
            aug[top + GROUP :, :] = aug[top + GROUP :, :] - taken[top + GROUP :, :]
        for step in steps.pop(0):
            step()


def panels_kernel(
    nrow, ncol, rows_here, cols_here,
    a, panel, left, right,
    p, ac, k, aug, low,
    psend, precv, zsend, ksend, ksib, krecv, asend, arecv, loc,
):
    chips = nrow // 2
    nx = math.isqrt(chips)
    ny = chips // nx
    nt = rows_here // NB
    na = cols_here // CW
    r = lax.axis_index("row")
    c = lax.axis_index("col")
    core = lax.rem(r, 2)
    q = r // 2
    qx = lax.rem(q, nx)
    qy = q // nx
    sib = r + 1 - 2 * core
    first = core == 0
    second = core == 1
    source = q == 0

    oy = lax.rem(qy, 2)
    ox = lax.rem(qx, 2)
    if nx > 1 and ny > 1:
        pos_x = qy * nx + qx + oy * (nx - 1 - 2 * qx)
        pos_y = qx * ny + qy + ox * (ny - 1 - 2 * qy)
        step_x = jnp.where(oy == 0, jnp.where(qx < nx - 1, 1, nx), jnp.where(qx > 0, -1, nx))
        step_y = jnp.where(ox == 0, jnp.where(qy < ny - 1, nx, 1), jnp.where(qy > 0, -nx, 1))
        pos = jnp.where(first, pos_x, pos_y)
        onward = lax.rem(r + 2 * jnp.where(first, step_x, step_y) + nrow, nrow)
    else:
        pos = q
        onward = lax.rem(r + 2, nrow)

    barrier = pltpu.get_barrier_semaphore()
    for i in range(1, ncol):
        pl.semaphore_signal(barrier, inc=1, device_id=(r, lax.rem(c + i, ncol)), device_id_type=MESH)
    for i in range(1, chips):
        pl.semaphore_signal(
            barrier, inc=1, device_id=(lax.rem(q + i, chips) * 2 + core, c), device_id_type=MESH
        )
    pl.semaphore_signal(barrier, inc=1, device_id=(sib, c), device_id_type=MESH)
    pl.semaphore_wait(barrier, ncol - 1 + chips)

    started = []

    def remote(src, dst, ss, rs, dev):
        return functools.partial(
            pltpu.make_async_remote_copy,
            src_ref=src, dst_ref=dst, send_sem=ss, recv_sem=rs, device_id=dev, device_id_type=MESH,
        )

    def start(cond, *makes):
        @pl.when(cond)
        def _():
            for make in makes:
                make().start()

        started.append((cond, makes))

    def incoming(dst, rs):
        return remote(dst, dst, loc.at[3], rs, (sib, c))

    def received(cond, *makes):
        @pl.when(cond)
        def _():
            for make in makes:
                make().wait_recv()

    def pc(s, t):
        return p.at[s, pl.ds(t * NB, NB)]

    def ach(s, t):
        return ac.at[s, :, pl.ds(t * CW, CW)]

    def a_rows(t):
        return a.at[pl.ds(t * NB, NB), pl.ds(0, NB)]

    def p_in(s, t):
        return incoming(pc(s, t), precv.at[s, t])

    def p_copy(s, t, src, z, way=0):
        return remote(src, pc(s, t), psend.at[s, t, way], precv.at[s, t], (r, z))

    def direct(s):
        return [
            remote(a_rows(0), pc(s, 0), zsend.at[i], precv.at[s, 0], (r, z))
            for i, z in enumerate([z for z in range(ncol - 1, -1, -1) if z != s])
        ]

    def spread(s, src):
        base = 0 if s == 0 else 1
        return [
            remote(src, k.at[s], ksend.at[s, j], krecv.at[s], (2 * j + base, c)) for j in range(chips - 1, 0, -1)
        ] + [remote(src, k.at[s], ksib.at[s], krecv.at[s], (sib, c))]

    def a_copies(t, src):
        over = remote(src, ach(core, t), asend.at[t, 0], arecv.at[core, t], (onward, c))
        across = remote(src, ach(core, t), asend.at[t, 1], arecv.at[core, t], (sib, c))
        return over, across

    def own(s):
        return pltpu.make_async_copy(a.at[:, pl.ds(0, NB)], p.at[s], loc.at[s])

    def own_slab():
        return pltpu.make_async_copy(a.at[pl.ds(0, NB), :], ac.at[core], loc.at[2])

    start((r == 0) & (c == 0), *direct(0))
    for s in range(2):
        pl.when(c == s)(own(s).start)
    rest = range(1, nt)

    def p_source(here, ts):
        start(here & (c == 0), *[p_copy(0, t, a_rows(t), 1) for t in ts])
        start(
            here & (c == 1),
            *[p_copy(1, t, a_rows(t), z, i) for t in ts for i, z in enumerate((0, 2) if ncol > 2 else (0,))],
        )

    received((r == 0) & (c != 0), p_in(0, 0))
    for s in range(2):
        pl.when(c == s)(own(s).wait)
    start(r == 0, *spread(0, pc(0, 0)))
    pl.when(source)(lambda: own_slab().start())
    p_source(q != 0, range(nt))
    received((q != 0) & first, incoming(k.at[0], krecv.at[0]))
    start((q != 0) & first, remote(k.at[0], k.at[0], ksib.at[0], krecv.at[0], (sib, c)))
    received(second, incoming(k.at[0], krecv.at[0]))

    def p_pass(t, z):
        here = (c == 1) if z == 1 else (c > 1) & (c < ncol - 1)
        if t == 0:
            here = here & (q != 0)
        panels = (0,) if z == 1 else (0, 1)
        received(here, *[p_in(s, t) for s in panels])
        start(here, *[p_copy(s, t, pc(s, t), c + 1) for s in panels])

    def direct_rest():
        start((r == 1) & (c == 0), *direct(0))
        start(source & (c == 1), *direct(1))

    def corner_rest():
        received((r == 1) & (c != 0), p_in(0, 0))
        received((r == 1) & (c != 1), p_in(1, 0))
        start(r == 1, *spread(1, pc(0, 0)), *spread(2, pc(1, 0)))

    def corner_pass():
        here = second & (q != 0)
        received(here, *[incoming(k.at[s], krecv.at[s]) for s in (1, 2)])
        start(here, *[remote(k.at[s], k.at[s], ksib.at[s], krecv.at[s], (sib, c)) for s in (1, 2)])

    def a_source():
        makes = [a_copies(t, a.at[pl.ds(0, NB), pl.ds(t * CW, CW)]) for t in range(na)]
        start(source, *[make for pair in makes for make in pair])

    def a_pass(t, at):
        here = pos == at if at < 3 else pos >= at
        over, across = a_copies(t, ach(core, t))
        received(here, incoming(ach(core, t), arecv.at[core, t]))
        if at < 3:
            start(here, over, across)
        else:
            start(here & (pos < chips - 1), over)
            start(here, across)

    half = NB // (2 * SUB)
    places = [[] for _ in range(2 * half)]

    def put(at, *step):
        places[min(int(at), 2 * half - 1)].append(functools.partial(*step))

    put(0, direct_rest)
    put(1, p_source, source, rest)
    put(1, a_source)
    put(2, corner_rest)
    put(5, corner_pass)
    for t in range(nt):
        if ncol > 2:
            put(1 + 2 * t, p_pass, t, 1)
        if ncol > 3:
            put(2 + 2 * t, p_pass, t, 2)
    for t in range(na):
        for at in range(1, min(chips, 4)):
            put(2 + 1.5 * t + 2 * (at - 1), a_pass, t, at)

    eye = jnp.where(
        lax.broadcasted_iota(jnp.int32, (NB, NB), 0) == lax.broadcasted_iota(jnp.int32, (NB, NB), 1),
        f32(1.0), f32(0.0),
    )

    @pl.when(r == 0)
    def _():
        aug[0, :, :NB] = p[0, :NB, :]

    @pl.when(r != 0)
    def _():
        aug[0, :, :NB] = k[0]

    aug[0, :, NB:] = eye
    eliminate(aug.at[0], places[:half])

    received(first, *[incoming(k.at[s], krecv.at[s]) for s in (1, 2)])

    @pl.when(r == 1)
    def _():
        k[1] = p[0, :NB, :]
        k[2] = p[1, :NB, :]

    w0 = aug[0, :, NB:]
    low[...] = dot(k[1], w0, 1, 1)
    l10 = low[...]
    aug[1, :, :NB] = k[2] - dot(l10, l10, 1, 1)
    aug[1, :, NB:] = eye
    eliminate(aug.at[1], places[half:])

    w1 = aug[1, :, NB:]
    w10 = -dot(w1, dot(l10, w0))
    w = jnp.concatenate(
        [jnp.concatenate([w0, jnp.zeros((NB, NB), f32)], axis=1), jnp.concatenate([w10, w1], axis=1)], axis=0
    )
    wh, wl = two(w)
    w_left = jnp.concatenate([wh, wl, wh], axis=1)
    wh, wl = two(w.T)
    w_right = jnp.concatenate([wh, wh, wl], axis=0)

    last = c == ncol - 1
    received(last & (c > 0), *[p_in(0, t) for t in rest])
    received((c == 0) | (last & (c > 1)), *[p_in(1, t) for t in rest])
    received((q != 0) & last, p_in(0, 0))
    received((q != 0) & ((c == 0) | (last & (c > 1))), p_in(1, 0))
    received((r == 0) & (c != 1), p_in(1, 0))
    pl.when(source)(lambda: own_slab().wait())

    rh0, rl0 = two(p[0])
    rh1, rl1 = two(p[1])
    rows = mm(jnp.concatenate([rh0, rh1, rl0, rl1, rh0, rh1], axis=1), w_right)
    panel[...] = rows
    rh, rl = two(rows)
    left[...] = jnp.concatenate([rh, rl, rh], axis=1)

    upper = lax.broadcasted_iota(jnp.int32, (NB, NB), 0) <= lax.broadcasted_iota(jnp.int32, (NB, NB), 1)

    @pl.when(r == 0)
    def _():
        panel[:NB, :NB] = jnp.where(upper, aug[0, :, :NB], f32(0.0)).T
        panel[:NB, NB:] = jnp.zeros((NB, NB), f32)

    @pl.when(r == 1)
    def _():
        panel[:NB, NB:] = jnp.where(upper, aug[1, :, :NB], f32(0.0)).T

    for t in range(na):
        incoming(ach(1 - core, t), arecv.at[1 - core, t])().wait_recv()
        here = slice(t * CW, (t + 1) * CW)
        h0, l0 = two(ac[0, :, here])
        h1, l1 = two(ac[1, :, here])
        cols = mm(w_left, jnp.concatenate([h0, h1, h0, h1, l0, l1], axis=0))
        ch, cl = two(cols)
        right[:, here] = jnp.concatenate([ch, ch, cl], axis=0)

    for cond, makes in started:
        @pl.when(cond)
        def _():
            for make in makes:
                make().wait_send()


def update_kernel(a, panel, left, right, out, held, sems):
    r = lax.axis_index("row")
    c = lax.axis_index("col")
    copies = []
    for t in range(a.shape[1] // TILE):
        here = pl.ds(t * TILE, TILE)
        held[:, here] = a[:, here] - mm(left[...], right[:, here])

        @pl.when(r < 2)
        def _():
            held[:NB, here] = jnp.zeros((NB, TILE), f32)

        if t == 0:
            for s in range(2):
                @pl.when(c == s)
                def _():
                    held[:, :NB] = panel[:, s * NB : (s + 1) * NB]

        copy = pltpu.make_async_copy(held.at[:, here], out.at[:, here], sems.at[t])
        copy.start()
        copies.append(copy)
    for copy in copies:
        copy.wait()


def local(nrow, ncol, kernel):
    rows, cols = kernel.shape
    nt = rows // NB
    na = cols // CW
    chips = nrow // 2
    dma = pltpu.SemaphoreType.DMA
    panel, left, right = pl.pallas_call(
        functools.partial(panels_kernel, nrow, ncol, rows, cols),
        out_shape=[
            jax.ShapeDtypeStruct((rows, 2 * NB), f32),
            jax.ShapeDtypeStruct((rows, 6 * NB), bf16),
            jax.ShapeDtypeStruct((6 * NB, cols), bf16),
        ],
        in_specs=[pl.BlockSpec(memory_space=pltpu.HBM)],
        out_specs=[pl.BlockSpec(memory_space=pltpu.VMEM)] * 3,
        scratch_shapes=[
            pltpu.VMEM((2, rows, NB), f32),
            pltpu.VMEM((2, NB, cols), f32),
            pltpu.VMEM((3, NB, NB), f32),
            pltpu.VMEM((2, NB, 2 * NB), f32),
            pltpu.VMEM((NB, NB), f32),
            dma((2, nt, 2)),
            dma((2, nt)),
            dma((ncol,)),
            dma((3, chips)),
            dma((3,)),
            dma((3,)),
            dma((na, 2)),
            dma((2, na)),
            dma((4,)),
        ],
        compiler_params=pltpu.CompilerParams(
            collective_id=0, has_side_effects=True, vmem_limit_bytes=48 * 1024 * 1024
        ),
        name="panels",
    )(kernel)
    return pl.pallas_call(
        update_kernel,
        out_shape=jax.ShapeDtypeStruct((rows, cols), f32),
        in_specs=[pl.BlockSpec(memory_space=pltpu.VMEM)] * 4,
        out_specs=pl.BlockSpec(memory_space=pltpu.HBM),
        scratch_shapes=[pltpu.VMEM((rows, cols), f32), pltpu.SemaphoreType.DMA((cols // TILE,))],
        compiler_params=pltpu.CompilerParams(vmem_limit_bytes=32 * 1024 * 1024),
        name="update",
    )(kernel, panel, left, right)


def solution(mesh):
    return jax.shard_map(
        functools.partial(local, mesh.shape["row"], mesh.shape["col"]),
        mesh=mesh,
        in_specs=(P("row", "col"),),
        out_specs=P("row", "col"),
        check_vma=False,
    )
```

```python
import functools
import math

import jax
import jax.numpy as jnp
from jax import lax
from jax.experimental import pallas as pl
from jax.experimental.pallas import tpu as pltpu
from jax.sharding import PartitionSpec as P

NB = 128
SUB = 8
GROUP = 16
CW = 256
TILE = 256
MESH = pl.DeviceIdType.MESH
f32 = jnp.float32
bf16 = jnp.bfloat16


def dot(a, b, ca=1, cb=0):
    return lax.dot_general(
        a,
        b,
        (((ca,), (cb,)), ((), ())),
        precision=lax.Precision.HIGHEST,
        preferred_element_type=f32,
    )


def split(x):
    h = x.astype(bf16).astype(f32)
    rest = x - h
    m = rest.astype(bf16).astype(f32)
    return h, m, rest - m


def two(x):
    h = x.astype(bf16)
    return h, (x - h.astype(f32)).astype(bf16)


def mm(a, b):
    return jnp.dot(a, b, preferred_element_type=f32)


def splat(x, lane):
    return jnp.broadcast_to(x[:, lane : lane + 1], (SUB, NB))


def eliminate(work):
    row = lax.broadcasted_iota(jnp.int32, (SUB, NB), 0)
    subs = GROUP // SUB
    rows = [
        [[jnp.broadcast_to(block[k : k + 1, h * NB : (h + 1) * NB], (SUB, NB)) for h in range(2)] for k in range(SUB)]
        for block in (work[s * SUB : (s + 1) * SUB, :] for s in range(subs))
    ]
    done = []
    for s in range(subs):
        mine = rows[s]
        wide = 2 * SUB if s + 1 < subs else SUB
        d = {(k, j): splat(mine[k][0], s * SUB + j) for k in range(SUB) for j in range(k, wide)}
        for j in range(SUB):
            inv = lax.rsqrt(d[j, j])
            for i in range(j + 1, wide):
                d[j, i] = d[j, i] * inv
            for i in range(j + 1, SUB):
                for l in range(i, wide):
                    d[i, l] = d[i, l] - d[j, i] * d[j, l]
            mine[j] = [x * inv for x in mine[j]]
            for i in range(j + 1, SUB):
                mine[i] = [x - d[j, i] * y for x, y in zip(mine[i], mine[j])]
        for later in range(s + 1, subs):
            for i in range(SUB):
                for k in range(SUB):
                    m = d[k, SUB + i] if later == s + 1 else splat(mine[k][0], later * SUB + i)
                    rows[later][i] = [x - m * y for x, y in zip(rows[later][i], mine[k])]
        halves = []
        for h in range(2):
            u = mine[0][h]
            for k in range(1, SUB):
                u = jnp.where(row == k, mine[k][h], u)
            halves.append(u)
        done.append(jnp.concatenate(halves, axis=1))
    u = jnp.concatenate(done, axis=0)
    h, m, l = split(u)
    left = jnp.concatenate([h, h, m, h, m, l], axis=0)[:, :NB].astype(bf16)
    right = jnp.concatenate([h, m, h, l, m, h], axis=0).astype(bf16)
    taken = lax.dot_general(left, right, (((0,), (0,)), ((), ())), preferred_element_type=f32)
    rest = work[GROUP:, :] - taken[GROUP:, :]
    work[: NB - GROUP, :NB] = pltpu.roll(rest[:, :NB], NB - GROUP, 1)
    work[: NB - GROUP, NB:] = rest[:, NB:]
    return u


def panels_kernel(
    nrow, ncol, rows_here, cols_here,
    a, panel, left, right,
    p, ac, k, aug, work, low,
    psend, precv, zsend, ksend, ksib, krecv, asend, arecv, loc,
):
    chips = nrow // 2
    nx = math.isqrt(chips)
    ny = chips // nx
    nt = rows_here // NB
    na = cols_here // CW
    r = lax.axis_index("row")
    c = lax.axis_index("col")
    core = lax.rem(r, 2)
    q = r // 2
    qx = lax.rem(q, nx)
    qy = q // nx
    sib = r + 1 - 2 * core
    first = core == 0
    second = core == 1
    source = q == 0

    oy = lax.rem(qy, 2)
    ox = lax.rem(qx, 2)
    if nx > 1 and ny > 1:
        pos_x = qy * nx + qx + oy * (nx - 1 - 2 * qx)
        pos_y = qx * ny + qy + ox * (ny - 1 - 2 * qy)
        step_x = jnp.where(oy == 0, jnp.where(qx < nx - 1, 1, nx), jnp.where(qx > 0, -1, nx))
        step_y = jnp.where(ox == 0, jnp.where(qy < ny - 1, nx, 1), jnp.where(qy > 0, -nx, 1))
        pos = jnp.where(first, pos_x, pos_y)
        onward = lax.rem(r + 2 * jnp.where(first, step_x, step_y) + nrow, nrow)
    else:
        pos = q
        onward = lax.rem(r + 2, nrow)

    barrier = pltpu.get_barrier_semaphore()
    for i in range(1, ncol):
        pl.semaphore_signal(barrier, inc=1, device_id=(r, lax.rem(c + i, ncol)), device_id_type=MESH)
    for i in range(1, chips):
        pl.semaphore_signal(
            barrier, inc=1, device_id=(lax.rem(q + i, chips) * 2 + core, c), device_id_type=MESH
        )
    pl.semaphore_signal(barrier, inc=1, device_id=(sib, c), device_id_type=MESH)
    pl.semaphore_wait(barrier, ncol - 1 + chips)

    ending = []

    def remote(src, dst, ss, rs, dev):
        return functools.partial(
            pltpu.make_async_remote_copy,
            src_ref=src, dst_ref=dst, send_sem=ss, recv_sem=rs, device_id=dev, device_id_type=MESH,
        )

    def start(cond, *makes):
        @pl.when(cond)
        def _():
            for make in makes:
                if ending:
                    make().wait_send()
                else:
                    make().start()

    def incoming(dst, rs):
        return remote(dst, dst, loc.at[3], rs, (sib, c))

    def received(cond, *makes):
        if ending:
            return

        @pl.when(cond)
        def _():
            for make in makes:
                make().wait_recv()

    def pc(s, t):
        return p.at[s, pl.ds(t * NB, NB)]

    def ach(s, t):
        return ac.at[s, :, pl.ds(t * CW, CW)]

    def a_rows(t):
        return a.at[pl.ds(t * NB, NB), pl.ds(0, NB)]

    def p_in(s, t):
        return incoming(pc(s, t), precv.at[s, t])

    def p_copy(s, t, src, z, way=0):
        return remote(src, pc(s, t), psend.at[s, t, way], precv.at[s, t], (r, z))

    def direct(s):
        return [
            remote(a_rows(0), pc(s, 0), zsend.at[i], precv.at[s, 0], (r, z))
            for i, z in enumerate([z for z in range(ncol - 1, -1, -1) if z != s])
        ]

    def spread(s, src):
        base = 0 if s == 0 else 1
        return [
            remote(src, k.at[s], ksend.at[s, j], krecv.at[s], (2 * j + base, c)) for j in range(chips - 1, 0, -1)
        ] + [remote(src, k.at[s], ksib.at[s], krecv.at[s], (sib, c))]

    def a_copies(t, src):
        over = remote(src, ach(core, t), asend.at[t, 0], arecv.at[core, t], (onward, c))
        across = remote(src, ach(core, t), asend.at[t, 1], arecv.at[core, t], (sib, c))
        return over, across

    def own(s):
        return pltpu.make_async_copy(a.at[:, pl.ds(0, NB)], p.at[s], loc.at[s])

    def own_slab():
        return pltpu.make_async_copy(a.at[pl.ds(0, NB), :], ac.at[core], loc.at[2])

    rest = range(1, nt)

    def p_source(here, ts):
        start(here & (c == 0), *[p_copy(0, t, a_rows(t), 1) for t in ts])
        start(
            here & (c == 1),
            *[p_copy(1, t, a_rows(t), z, i) for t in ts for i, z in enumerate((0, 2) if ncol > 2 else (0,))],
        )

    def opening():
        start((r == 0) & (c == 0), *direct(0))
        if not ending:
            for s in range(2):
                pl.when(c == s)(own(s).start)
        received((r == 0) & (c != 0), p_in(0, 0))
        if not ending:
            for s in range(2):
                pl.when(c == s)(own(s).wait)
        start(r == 0, *spread(0, pc(0, 0)))
        p_source(q != 0, range(nt))
        received((q != 0) & first, incoming(k.at[0], krecv.at[0]))
        start((q != 0) & first, remote(k.at[0], k.at[0], ksib.at[0], krecv.at[0], (sib, c)))
        received(second, incoming(k.at[0], krecv.at[0]))
        if not ending:
            pl.when(source)(lambda: own_slab().start())

    def p_pass(t, z):
        here = (c == 1) if z == 1 else (c > 1) & (c < ncol - 1)
        if t == 0:
            here = here & (q != 0)
        panels = (0,) if z == 1 else (0, 1)
        received(here, *[p_in(s, t) for s in panels])
        start(here, *[p_copy(s, t, pc(s, t), c + 1) for s in panels])

    def direct_rest():
        start((r == 1) & (c == 0), *direct(0))
        start(source & (c == 1), *direct(1))

    def corner_rest():
        received((r == 1) & (c != 0), p_in(0, 0))
        received((r == 1) & (c != 1), p_in(1, 0))
        start(r == 1, *spread(1, pc(0, 0)), *spread(2, pc(1, 0)))

    def corner_pass():
        here = second & (q != 0)
        received(here, *[incoming(k.at[s], krecv.at[s]) for s in (1, 2)])
        start(here, *[remote(k.at[s], k.at[s], ksib.at[s], krecv.at[s], (sib, c)) for s in (1, 2)])

    def a_source():
        makes = [a_copies(t, a.at[pl.ds(0, NB), pl.ds(t * CW, CW)]) for t in range(na)]
        start(source, *[make for pair in makes for make in pair])

    def a_pass(t, at):
        here = pos == at if at < 3 else pos >= at
        over, across = a_copies(t, ach(core, t))
        received(here, incoming(ach(core, t), arecv.at[core, t]))
        if at < 3:
            start(here, over, across)
        else:
            start(here & (pos < chips - 1), over)
            start(here, across)

    half = NB // GROUP
    places = [[] for _ in range(2 * half)]

    def put(at, *step):
        places[min(int(at), 2 * half - 1)].append(functools.partial(*step))

    put(0, direct_rest)
    put(1, p_source, source, rest)
    put(1, a_source)
    put(2, corner_rest)
    put(5, corner_pass)
    for t in range(nt):
        if ncol > 2:
            put(1 + 2 * t, p_pass, t, 1)
        if ncol > 3:
            put(2 + 2 * t, p_pass, t, 2)
    for t in range(na):
        for at in range(1, min(chips, 4)):
            put(2 + 1.5 * t + 2 * (at - 1), a_pass, t, at)

    opening()

    eye = jnp.where(
        lax.broadcasted_iota(jnp.int32, (NB, NB), 0) == lax.broadcasted_iota(jnp.int32, (NB, NB), 1),
        f32(1.0), f32(0.0),
    )

    @pl.when(r == 0)
    def _():
        work[:, :NB] = p[0, :NB, :]

    @pl.when(r != 0)
    def _():
        work[:, :NB] = k[0]

    work[:, NB:] = eye

    def second_block():
        received(first, *[incoming(k.at[s], krecv.at[s]) for s in (1, 2)])

        @pl.when(r == 1)
        def _():
            k[1] = p[0, :NB, :]
            k[2] = p[1, :NB, :]

        l10 = dot(k[1], aug[0, :, NB:], 1, 1)
        low[...] = l10
        work[:, :NB] = k[2] - dot(l10, l10, 1, 1)
        work[:, NB:] = eye

    def group(g, carry):
        pl.when(g == half)(second_block)
        u = eliminate(work)
        h = g // half
        top = lax.rem(g, half) * GROUP
        here = pl.ds(pl.multiple_of(top, GROUP), GROUP)
        aug[h, here, :NB] = pltpu.roll(u[:, :NB], top, 1)
        aug[h, here, NB:] = u[:, NB:]
        for at, steps in enumerate(places):
            if steps:
                @pl.when(g == at)
                def _():
                    for step in steps:
                        step()
        return carry

    lax.fori_loop(0, 2 * half, group, 0)
    w0 = aug[0, :, NB:]
    l10 = low[...]

    w1 = aug[1, :, NB:]
    w10 = -dot(w1, dot(l10, w0))
    w = jnp.concatenate(
        [jnp.concatenate([w0, jnp.zeros((NB, NB), f32)], axis=1), jnp.concatenate([w10, w1], axis=1)], axis=0
    )
    wh, wl = two(w)
    w_left = jnp.concatenate([wh, wl, wh], axis=1)
    wh, wl = two(w.T)
    w_right = jnp.concatenate([wh, wh, wl], axis=0)

    last = c == ncol - 1
    received(last & (c > 0), *[p_in(0, t) for t in rest])
    received((c == 0) | (last & (c > 1)), *[p_in(1, t) for t in rest])
    received((q != 0) & last, p_in(0, 0))
    received((q != 0) & ((c == 0) | (last & (c > 1))), p_in(1, 0))
    received((r == 0) & (c != 1), p_in(1, 0))
    pl.when(source)(lambda: own_slab().wait())

    def rows_part(t, carry):
        here = pl.ds(pl.multiple_of(t * NB, NB), NB)
        rh0, rl0 = two(p[0, here, :])
        rh1, rl1 = two(p[1, here, :])
        rows = mm(jnp.concatenate([rh0, rh1, rl0, rl1, rh0, rh1], axis=1), w_right)
        panel[here, :] = rows
        rh, rl = two(rows)
        left[here, :] = jnp.concatenate([rh, rl, rh], axis=1)
        return carry

    lax.fori_loop(0, nt, rows_part, 0)

    upper = lax.broadcasted_iota(jnp.int32, (NB, NB), 0) <= lax.broadcasted_iota(jnp.int32, (NB, NB), 1)

    @pl.when(r == 0)
    def _():
        panel[:NB, :NB] = jnp.where(upper, aug[0, :, :NB], f32(0.0)).T
        panel[:NB, NB:] = jnp.zeros((NB, NB), f32)

    @pl.when(r == 1)
    def _():
        panel[:NB, NB:] = jnp.where(upper, aug[1, :, :NB], f32(0.0)).T

    def cols_part(t, carry):
        here = pl.ds(pl.multiple_of(t * CW, CW), CW)
        incoming(ac.at[1 - core, :, here], arecv.at[1 - core, t])().wait_recv()
        h0, l0 = two(ac[0, :, here])
        h1, l1 = two(ac[1, :, here])
        cols = mm(w_left, jnp.concatenate([h0, h1, h0, h1, l0, l1], axis=0))
        ch, cl = two(cols)
        right[:, here] = jnp.concatenate([ch, ch, cl], axis=0)
        return carry

    lax.fori_loop(0, na, cols_part, 0)

    ending.append(True)
    opening()
    for steps in places:
        for step in steps:
            step()


def update_kernel(a, panel, left, right, out, held, sems):
    r = lax.axis_index("row")
    c = lax.axis_index("col")

    def copy(t):
        here = pl.ds(pl.multiple_of(t * TILE, TILE), TILE)
        return pltpu.make_async_copy(held.at[:, here], out.at[:, here], sems.at[t])

    def tile(t, carry):
        here = pl.ds(pl.multiple_of(t * TILE, TILE), TILE)
        held[:, here] = a[:, here] - mm(left[...], right[:, here])

        @pl.when(r < 2)
        def _():
            held[:NB, here] = jnp.zeros((NB, TILE), f32)

        for s in range(2):
            @pl.when((t == 0) & (c == s))
            def _():
                held[:, :NB] = panel[:, s * NB : (s + 1) * NB]

        copy(t).start()
        return carry

    tiles = a.shape[1] // TILE
    lax.fori_loop(0, tiles, tile, 0)
    for t in range(tiles):
        copy(t).wait()


def local(nrow, ncol, kernel):
    rows, cols = kernel.shape
    nt = rows // NB
    na = cols // CW
    chips = nrow // 2
    dma = pltpu.SemaphoreType.DMA
    panel, left, right = pl.pallas_call(
        functools.partial(panels_kernel, nrow, ncol, rows, cols),
        out_shape=[
            jax.ShapeDtypeStruct((rows, 2 * NB), f32),
            jax.ShapeDtypeStruct((rows, 6 * NB), bf16),
            jax.ShapeDtypeStruct((6 * NB, cols), bf16),
        ],
        in_specs=[pl.BlockSpec(memory_space=pltpu.HBM)],
        out_specs=[pl.BlockSpec(memory_space=pltpu.VMEM)] * 3,
        scratch_shapes=[
            pltpu.VMEM((2, rows, NB), f32),
            pltpu.VMEM((2, NB, cols), f32),
            pltpu.VMEM((3, NB, NB), f32),
            pltpu.VMEM((2, NB, 2 * NB), f32),
            pltpu.VMEM((NB, 2 * NB), f32),
            pltpu.VMEM((NB, NB), f32),
            dma((2, nt, 2)),
            dma((2, nt)),
            dma((ncol,)),
            dma((3, chips)),
            dma((3,)),
            dma((3,)),
            dma((na, 2)),
            dma((2, na)),
            dma((4,)),
        ],
        compiler_params=pltpu.CompilerParams(
            collective_id=0, has_side_effects=True, vmem_limit_bytes=48 * 1024 * 1024
        ),
        name="panels",
    )(kernel)
    return pl.pallas_call(
        update_kernel,
        out_shape=jax.ShapeDtypeStruct((rows, cols), f32),
        in_specs=[pl.BlockSpec(memory_space=pltpu.VMEM)] * 4,
        out_specs=pl.BlockSpec(memory_space=pltpu.HBM),
        scratch_shapes=[pltpu.VMEM((rows, cols), f32), pltpu.SemaphoreType.DMA((cols // TILE,))],
        compiler_params=pltpu.CompilerParams(vmem_limit_bytes=32 * 1024 * 1024),
        name="update",
    )(kernel, panel, left, right)


def solution(mesh):
    return jax.shard_map(
        functools.partial(local, mesh.shape["row"], mesh.shape["col"]),
        mesh=mesh,
        in_specs=(P("row", "col"),),
        out_specs=P("row", "col"),
        check_vma=False,
    )
```

```python
import functools
import math

import jax
import jax.numpy as jnp
from jax import lax
from jax.experimental import pallas as pl
from jax.experimental.pallas import tpu as pltpu
from jax.sharding import PartitionSpec as P

NB = 128
SUB = 8
GROUP = 32
CW = 256
TILE = 256
MESH = pl.DeviceIdType.MESH
f32 = jnp.float32
bf16 = jnp.bfloat16


def dot(a, b, ca=1, cb=0):
    return lax.dot_general(
        a,
        b,
        (((ca,), (cb,)), ((), ())),
        precision=lax.Precision.HIGHEST,
        preferred_element_type=f32,
    )


def split(x):
    h = x.astype(bf16).astype(f32)
    rest = x - h
    m = rest.astype(bf16).astype(f32)
    return h, m, rest - m


def two(x):
    h = x.astype(bf16)
    return h, (x - h.astype(f32)).astype(bf16)


def mm(a, b):
    return jnp.dot(a, b, preferred_element_type=f32)


def splat(x, lane):
    return jnp.broadcast_to(x[:, lane : lane + 1], (SUB, NB))


def eliminate(work, midway):
    row = lax.broadcasted_iota(jnp.int32, (SUB, NB), 0)
    subs = GROUP // SUB
    rows = [
        [[jnp.broadcast_to(block[k : k + 1, h * NB : (h + 1) * NB], (SUB, NB)) for h in range(2)] for k in range(SUB)]
        for block in (work[s * SUB : (s + 1) * SUB, :] for s in range(subs))
    ]
    done = []
    for s in range(subs):
        mine = rows[s]
        wide = 2 * SUB if s + 1 < subs else SUB
        d = {(k, j): splat(mine[k][0], s * SUB + j) for k in range(SUB) for j in range(k, wide)}
        for j in range(SUB):
            inv = lax.rsqrt(d[j, j])
            for i in range(j + 1, wide):
                d[j, i] = d[j, i] * inv
            for i in range(j + 1, SUB):
                for l in range(i, wide):
                    d[i, l] = d[i, l] - d[j, i] * d[j, l]
            mine[j] = [x * inv for x in mine[j]]
            for i in range(j + 1, SUB):
                mine[i] = [x - d[j, i] * y for x, y in zip(mine[i], mine[j])]
        for later in range(s + 1, subs):
            for i in range(SUB):
                for k in range(SUB):
                    m = d[k, SUB + i] if later == s + 1 else splat(mine[k][0], later * SUB + i)
                    rows[later][i] = [x - m * y for x, y in zip(rows[later][i], mine[k])]
        halves = []
        for h in range(2):
            u = mine[0][h]
            for k in range(1, SUB):
                u = jnp.where(row == k, mine[k][h], u)
            halves.append(u)
        done.append(jnp.concatenate(halves, axis=1))
        if s == subs // 2 - 1:
            midway()
    u = jnp.concatenate(done, axis=0)
    h, m, l = split(u)
    left = jnp.concatenate([h, h, m, h, m, l], axis=0)[:, :NB].astype(bf16)
    right = jnp.concatenate([h, m, h, l, m, h], axis=0).astype(bf16)
    taken = lax.dot_general(left, right, (((0,), (0,)), ((), ())), preferred_element_type=f32)
    rest = work[GROUP:, :] - taken[GROUP:, :]
    work[: NB - GROUP, :NB] = pltpu.roll(rest[:, :NB], NB - GROUP, 1)
    work[: NB - GROUP, NB:] = rest[:, NB:]
    return u


def panels_kernel(
    nrow, ncol, rows_here, cols_here,
    a, panel, left, right,
    p, ac, k, aug, work, low,
    psend, precv, zsend, ksend, ksib, krecv, asend, arecv, slab, loc,
):
    chips = nrow // 2
    nx = math.isqrt(chips)
    ny = chips // nx
    nt = rows_here // NB
    na = cols_here // CW
    r = lax.axis_index("row")
    c = lax.axis_index("col")
    core = lax.rem(r, 2)
    q = r // 2
    qx = lax.rem(q, nx)
    qy = q // nx
    sib = r + 1 - 2 * core
    first = core == 0
    second = core == 1
    source = q == 0

    oy = lax.rem(qy, 2)
    ox = lax.rem(qx, 2)
    if nx > 1 and ny > 1:
        pos_x = qy * nx + qx + oy * (nx - 1 - 2 * qx)
        pos_y = qx * ny + qy + ox * (ny - 1 - 2 * qy)
        step_x = jnp.where(oy == 0, jnp.where(qx < nx - 1, 1, nx), jnp.where(qx > 0, -1, nx))
        step_y = jnp.where(ox == 0, jnp.where(qy < ny - 1, nx, 1), jnp.where(qy > 0, -nx, 1))
        pos = jnp.where(first, pos_x, pos_y)
        onward = lax.rem(r + 2 * jnp.where(first, step_x, step_y) + nrow, nrow)
    else:
        pos = q
        onward = lax.rem(r + 2, nrow)

    barrier = pltpu.get_barrier_semaphore()
    for i in range(1, ncol):
        pl.semaphore_signal(barrier, inc=1, device_id=(r, lax.rem(c + i, ncol)), device_id_type=MESH)
    for i in range(1, chips):
        pl.semaphore_signal(
            barrier, inc=1, device_id=(lax.rem(q + i, chips) * 2 + core, c), device_id_type=MESH
        )
    pl.semaphore_signal(barrier, inc=1, device_id=(sib, c), device_id_type=MESH)
    pl.semaphore_wait(barrier, ncol - 1 + chips)

    ending = []

    def remote(src, dst, ss, rs, dev):
        return functools.partial(
            pltpu.make_async_remote_copy,
            src_ref=src, dst_ref=dst, send_sem=ss, recv_sem=rs, device_id=dev, device_id_type=MESH,
        )

    def start(cond, *makes):
        @pl.when(cond)
        def _():
            for make in makes:
                if ending:
                    make().wait_send()
                else:
                    make().start()

    def incoming(dst, rs):
        return remote(dst, dst, loc.at[3], rs, (sib, c))

    def received(cond, *makes):
        if ending:
            return

        @pl.when(cond)
        def _():
            for make in makes:
                make().wait_recv()

    def pc(s, t):
        return p.at[s, pl.ds(t * NB, NB)]

    def ach(s, t):
        return ac.at[s, t]

    def a_rows(t):
        return a.at[pl.ds(t * NB, NB), pl.ds(0, NB)]

    def p_in(s, t):
        return incoming(pc(s, t), precv.at[s, t])

    def p_copy(s, t, src, z, way=0):
        return remote(src, pc(s, t), psend.at[s, t, way], precv.at[s, t], (r, z))

    def direct(s):
        return [
            remote(a_rows(0), pc(s, 0), zsend.at[i], precv.at[s, 0], (r, z))
            for i, z in enumerate([z for z in range(ncol - 1, -1, -1) if z != s])
        ]

    def spread(s, src):
        base = 0 if s == 0 else 1
        return [remote(src, k.at[s], ksib.at[s], krecv.at[s], (sib, c))] + [
            remote(src, k.at[s], ksend.at[s, j], krecv.at[s], (2 * j + base, c)) for j in range(chips - 1, 0, -1)
        ]

    def a_copies(t, src):
        over = remote(src, ach(core, t), asend.at[t, 0], arecv.at[core, t], (onward, c))
        across = remote(src, ach(core, t), asend.at[t, 1], arecv.at[core, t], (sib, c))
        return over, across

    def own(s):
        return pltpu.make_async_copy(a.at[:, pl.ds(0, NB)], p.at[s], loc.at[s])

    def own_slab():
        return [
            pltpu.make_async_copy(a.at[pl.ds(0, NB), pl.ds(t * CW, CW)], ach(core, t), slab.at[t]) for t in range(na)
        ]

    rest = range(1, nt)

    def p_source(here, ts):
        start(here & (c == 0), *[p_copy(0, t, pc(0, t), 1) for t in ts])
        start(
            here & (c == 1),
            *[p_copy(1, t, pc(1, t), z, i) for t in ts for i, z in enumerate((0, 2) if ncol > 2 else (0,))],
        )

    def opening():
        start((r == 0) & (c == 0), *direct(0))
        if not ending:
            for s in range(2):
                pl.when(c == s)(own(s).start)
        received((r == 0) & (c != 0), p_in(0, 0))
        if not ending:
            for s in range(2):
                pl.when(c == s)(own(s).wait)
        start(r == 0, *spread(0, pc(0, 0)))
        p_source(q != 0, range(nt))
        received((q != 0) & first, incoming(k.at[0], krecv.at[0]))
        start((q != 0) & first, remote(k.at[0], k.at[0], ksib.at[0], krecv.at[0], (sib, c)))
        received(second, incoming(k.at[0], krecv.at[0]))
        if not ending:
            pl.when(source)(lambda: [copy.start() for copy in own_slab()] and None)

    def p_pass(t, z):
        here = (c == 1) if z == 1 else (c > 1) & (c < ncol - 1)
        if t == 0:
            here = here & (q != 0)
        panels = (0,) if z == 1 else (0, 1)
        received(here, *[p_in(s, t) for s in panels])
        start(here, *[p_copy(s, t, pc(s, t), c + 1) for s in panels])

    def direct_rest():
        start((r == 1) & (c == 0), *direct(0))
        start((r == 1) & (c == 1), *direct(1))

    def corner_rest():
        received((r == 1) & (c != 0), p_in(0, 0))
        received((r == 1) & (c != 1), p_in(1, 0))
        start(r == 1, *spread(1, pc(0, 0)), *spread(2, pc(1, 0)))

    def corner_pass():
        here = second & (q != 0)
        received(here, *[incoming(k.at[s], krecv.at[s]) for s in (1, 2)])
        start(here, *[remote(k.at[s], k.at[s], ksib.at[s], krecv.at[s], (sib, c)) for s in (1, 2)])

    def a_source():
        if not ending:
            pl.when(source)(lambda: [copy.wait() for copy in own_slab()] and None)
        makes = [a_copies(t, ach(core, t)) for t in range(na)]
        start(source, *[make for pair in makes for make in pair])

    def a_pass(t, at):
        here = pos == at if at < 3 else pos >= at
        over, across = a_copies(t, ach(core, t))
        received(here, incoming(ach(core, t), arecv.at[core, t]))
        if at < 3:
            start(here, over, across)
        else:
            start(here & (pos < chips - 1), over)
            start(here, across)

    half = NB // GROUP
    places = [[] for _ in range(4 * half)]

    def put(at, *step):
        places[min(int(at), 4 * half - 1)].append(functools.partial(*step))

    put(0, direct_rest)
    put(1, p_source, source, rest)
    put(0, a_source)
    put(2, corner_rest)
    put(5, corner_pass)
    for t in range(nt):
        if ncol > 2:
            put(1 + 2 * t, p_pass, t, 1)
        if ncol > 3:
            put(2 + 2 * t, p_pass, t, 2)
    for t in range(na):
        for at in range(1, min(chips, 4)):
            put(2 + 1.5 * t + 2 * (at - 1), a_pass, t, at)

    opening()

    eye = jnp.where(
        lax.broadcasted_iota(jnp.int32, (NB, NB), 0) == lax.broadcasted_iota(jnp.int32, (NB, NB), 1),
        f32(1.0), f32(0.0),
    )

    @pl.when(r == 0)
    def _():
        work[:, :NB] = p[0, :NB, :]

    @pl.when(r != 0)
    def _():
        work[:, :NB] = k[0]

    work[:, NB:] = eye

    def second_block():
        received(first, *[incoming(k.at[s], krecv.at[s]) for s in (1, 2)])

        @pl.when(r == 1)
        def _():
            k[1] = p[0, :NB, :]
            k[2] = p[1, :NB, :]

        l10 = dot(k[1], aug[0, :, NB:], 1, 1)
        low[...] = l10
        work[:, :NB] = k[2] - dot(l10, l10, 1, 1)
        work[:, NB:] = eye

    def group(g, carry):
        pl.when(g == half)(second_block)

        def visit(odd):
            for at, steps in enumerate(places):
                if steps and at % 2 == odd:
                    @pl.when(g == at // 2)
                    def _():
                        for step in steps:
                            step()

        u = eliminate(work, functools.partial(visit, 0))
        h = g // half
        top = lax.rem(g, half) * GROUP
        here = pl.ds(pl.multiple_of(top, GROUP), GROUP)
        aug[h, here, :NB] = pltpu.roll(u[:, :NB], top, 1)
        aug[h, here, NB:] = u[:, NB:]
        visit(1)
        return carry

    lax.fori_loop(0, 2 * half, group, 0)
    w0 = aug[0, :, NB:]
    l10 = low[...]

    w1 = aug[1, :, NB:]
    w10 = -dot(w1, dot(l10, w0))
    w = jnp.concatenate(
        [jnp.concatenate([w0, jnp.zeros((NB, NB), f32)], axis=1), jnp.concatenate([w10, w1], axis=1)], axis=0
    )
    wh, wl = two(w)
    w_left = jnp.concatenate([wh, wl, wh], axis=1)
    wh, wl = two(w.T)
    w_right = jnp.concatenate([wh, wh, wl], axis=0)

    last = c == ncol - 1
    received(last & (c > 0), *[p_in(0, t) for t in rest])
    received((c == 0) | (last & (c > 1)), *[p_in(1, t) for t in rest])
    received((q != 0) & last, p_in(0, 0))
    received((q != 0) & ((c == 0) | (last & (c > 1))), p_in(1, 0))

    def rows_part(t, carry):
        here = pl.ds(pl.multiple_of(t * NB, NB), NB)
        rh0, rl0 = two(p[0, here, :])
        rh1, rl1 = two(p[1, here, :])
        rows = mm(jnp.concatenate([rh0, rh1, rl0, rl1, rh0, rh1], axis=1), w_right)
        panel[here, :] = rows
        rh, rl = two(rows)
        left[here, :] = jnp.concatenate([rh, rl, rh], axis=1)
        return carry

    lax.fori_loop(0, nt, rows_part, 0)

    upper = lax.broadcasted_iota(jnp.int32, (NB, NB), 0) <= lax.broadcasted_iota(jnp.int32, (NB, NB), 1)

    @pl.when(r == 0)
    def _():
        panel[:NB, :NB] = jnp.where(upper, aug[0, :, :NB], f32(0.0)).T
        panel[:NB, NB:] = jnp.zeros((NB, NB), f32)

    @pl.when(r == 1)
    def _():
        panel[:NB, NB:] = jnp.where(upper, aug[1, :, :NB], f32(0.0)).T

    def cols_part(t, carry):
        here = pl.ds(pl.multiple_of(t * CW, CW), CW)
        incoming(ac.at[1 - core, t], arecv.at[1 - core, t])().wait_recv()
        h0, l0 = two(ac[0, t])
        h1, l1 = two(ac[1, t])
        cols = mm(w_left, jnp.concatenate([h0, h1, h0, h1, l0, l1], axis=0))
        ch, cl = two(cols)
        right[:, here] = jnp.concatenate([ch, ch, cl], axis=0)
        return carry

    lax.fori_loop(0, na, cols_part, 0)

    ending.append(True)
    opening()
    for steps in places:
        for step in steps:
            step()


def update_kernel(a, panel, left, right, out, held, sems):
    r = lax.axis_index("row")
    c = lax.axis_index("col")

    def copy(t):
        here = pl.ds(pl.multiple_of(t * TILE, TILE), TILE)
        return pltpu.make_async_copy(held.at[:, here], out.at[:, here], sems.at[t])

    def tile(t, carry):
        here = pl.ds(pl.multiple_of(t * TILE, TILE), TILE)
        held[:, here] = a[:, here] - mm(left[...], right[:, here])

        @pl.when(r < 2)
        def _():
            held[:NB, here] = jnp.zeros((NB, TILE), f32)

        for s in range(2):
            @pl.when((t == 0) & (c == s))
            def _():
                held[:, :NB] = panel[:, s * NB : (s + 1) * NB]

        copy(t).start()
        return carry

    tiles = a.shape[1] // TILE
    lax.fori_loop(0, tiles, tile, 0)
    for t in range(tiles):
        copy(t).wait()


def local(nrow, ncol, kernel):
    rows, cols = kernel.shape
    nt = rows // NB
    na = cols // CW
    chips = nrow // 2
    dma = pltpu.SemaphoreType.DMA
    panel, left, right = pl.pallas_call(
        functools.partial(panels_kernel, nrow, ncol, rows, cols),
        out_shape=[
            jax.ShapeDtypeStruct((rows, 2 * NB), f32),
            jax.ShapeDtypeStruct((rows, 6 * NB), bf16),
            jax.ShapeDtypeStruct((6 * NB, cols), bf16),
        ],
        in_specs=[pl.BlockSpec(memory_space=pltpu.HBM)],
        out_specs=[pl.BlockSpec(memory_space=pltpu.VMEM)] * 3,
        scratch_shapes=[
            pltpu.VMEM((2, rows, NB), f32),
            pltpu.VMEM((2, na, NB, CW), f32),
            pltpu.VMEM((3, NB, NB), f32),
            pltpu.VMEM((2, NB, 2 * NB), f32),
            pltpu.VMEM((NB, 2 * NB), f32),
            pltpu.VMEM((NB, NB), f32),
            dma((2, nt, 2)),
            dma((2, nt)),
            dma((ncol,)),
            dma((3, chips)),
            dma((3,)),
            dma((3,)),
            dma((na, 2)),
            dma((2, na)),
            dma((na,)),
            dma((4,)),
        ],
        compiler_params=pltpu.CompilerParams(
            collective_id=0, has_side_effects=True, vmem_limit_bytes=48 * 1024 * 1024
        ),
        name="panels",
    )(kernel)
    return pl.pallas_call(
        update_kernel,
        out_shape=jax.ShapeDtypeStruct((rows, cols), f32),
        in_specs=[pl.BlockSpec(memory_space=pltpu.VMEM)] * 4,
        out_specs=pl.BlockSpec(memory_space=pltpu.HBM),
        scratch_shapes=[pltpu.VMEM((rows, cols), f32), pltpu.SemaphoreType.DMA((cols // TILE,))],
        compiler_params=pltpu.CompilerParams(vmem_limit_bytes=32 * 1024 * 1024),
        name="update",
    )(kernel, panel, left, right)


def solution(mesh):
    return jax.shard_map(
        functools.partial(local, mesh.shape["row"], mesh.shape["col"]),
        mesh=mesh,
        in_specs=(P("row", "col"),),
        out_specs=P("row", "col"),
        check_vma=False,
    )
```

```python
import functools
import math

import jax
import jax.numpy as jnp
from jax import lax
from jax.experimental import pallas as pl
from jax.experimental.pallas import tpu as pltpu
from jax.sharding import PartitionSpec as P

NB = 128
SUB = 8
GROUP = 32
CW = 256
TILE = 256
MESH = pl.DeviceIdType.MESH
f32 = jnp.float32
bf16 = jnp.bfloat16


def dot(a, b, ca=1, cb=0):
    return lax.dot_general(
        a,
        b,
        (((ca,), (cb,)), ((), ())),
        precision=lax.Precision.HIGHEST,
        preferred_element_type=f32,
    )


def split(x):
    h = x.astype(bf16).astype(f32)
    rest = x - h
    m = rest.astype(bf16).astype(f32)
    return h, m, rest - m


def two(x):
    h = x.astype(bf16)
    return h, (x - h.astype(f32)).astype(bf16)


def mm(a, b):
    return jnp.dot(a, b, preferred_element_type=f32)


def splat(x, lane):
    return jnp.broadcast_to(x[:, lane : lane + 1], (SUB, NB))


def eliminate(work, midway):
    row = lax.broadcasted_iota(jnp.int32, (SUB, NB), 0)
    subs = GROUP // SUB
    rows = [
        [[jnp.broadcast_to(block[k : k + 1, h * NB : (h + 1) * NB], (SUB, NB)) for h in range(2)] for k in range(SUB)]
        for block in (work[s * SUB : (s + 1) * SUB, :] for s in range(subs))
    ]
    done = []
    for s in range(subs):
        mine = rows[s]
        wide = 2 * SUB if s + 1 < subs else SUB
        d = {(k, j): splat(mine[k][0], s * SUB + j) for k in range(SUB) for j in range(k, wide)}
        for j in range(SUB):
            inv = lax.rsqrt(d[j, j])
            for i in range(j + 1, wide):
                d[j, i] = d[j, i] * inv
            for i in range(j + 1, SUB):
                for l in range(i, wide):
                    d[i, l] = d[i, l] - d[j, i] * d[j, l]
            mine[j] = [x * inv for x in mine[j]]
            for i in range(j + 1, SUB):
                mine[i] = [x - d[j, i] * y for x, y in zip(mine[i], mine[j])]
        for later in range(s + 1, subs):
            for i in range(SUB):
                for k in range(SUB):
                    m = d[k, SUB + i] if later == s + 1 else splat(mine[k][0], later * SUB + i)
                    rows[later][i] = [x - m * y for x, y in zip(rows[later][i], mine[k])]
        halves = []
        for h in range(2):
            u = mine[0][h]
            for k in range(1, SUB):
                u = jnp.where(row == k, mine[k][h], u)
            halves.append(u)
        done.append(jnp.concatenate(halves, axis=1))
        if s == subs // 2 - 1:
            midway()
    u = jnp.concatenate(done, axis=0)
    h, m, l = split(u)
    left = jnp.concatenate([h, h, m, h, m, l], axis=0)[:, :NB].astype(bf16)
    right = jnp.concatenate([h, m, h, l, m, h], axis=0).astype(bf16)
    taken = lax.dot_general(left, right, (((0,), (0,)), ((), ())), preferred_element_type=f32)
    rest = work[GROUP:, :] - taken[GROUP:, :]
    work[: NB - GROUP, :NB] = pltpu.roll(rest[:, :NB], NB - GROUP, 1)
    work[: NB - GROUP, NB:] = rest[:, NB:]
    return u


def panels_kernel(
    nrow, ncol, rows_here, cols_here,
    a, panel, left, right,
    p, ac, k, aug, work, low,
    psend, precv, zsend, ksend, ksib, krecv, asend, arecv, slab, loc,
):
    chips = nrow // 2
    nx = math.isqrt(chips)
    ny = chips // nx
    nt = rows_here // NB
    na = cols_here // CW
    r = lax.axis_index("row")
    c = lax.axis_index("col")
    core = lax.rem(r, 2)
    q = r // 2
    qx = lax.rem(q, nx)
    qy = q // nx
    sib = r + 1 - 2 * core
    first = core == 0
    second = core == 1
    source = q == 0

    oy = lax.rem(qy, 2)
    ox = lax.rem(qx, 2)
    if nx > 1 and ny > 1:
        pos_x = qy * nx + qx + oy * (nx - 1 - 2 * qx)
        pos_y = qx * ny + qy + ox * (ny - 1 - 2 * qy)
        step_x = jnp.where(oy == 0, jnp.where(qx < nx - 1, 1, nx), jnp.where(qx > 0, -1, nx))
        step_y = jnp.where(ox == 0, jnp.where(qy < ny - 1, nx, 1), jnp.where(qy > 0, -nx, 1))
        pos = jnp.where(first, pos_x, pos_y)
        onward = lax.rem(r + 2 * jnp.where(first, step_x, step_y) + nrow, nrow)
    else:
        pos = q
        onward = lax.rem(r + 2, nrow)

    barrier = pltpu.get_barrier_semaphore()
    for i in range(1, ncol):
        pl.semaphore_signal(barrier, inc=1, device_id=(r, lax.rem(c + i, ncol)), device_id_type=MESH)
    for i in range(1, chips):
        pl.semaphore_signal(
            barrier, inc=1, device_id=(lax.rem(q + i, chips) * 2 + core, c), device_id_type=MESH
        )
    pl.semaphore_signal(barrier, inc=1, device_id=(sib, c), device_id_type=MESH)
    pl.semaphore_wait(barrier, ncol - 1 + chips)

    ending = []

    def remote(src, dst, ss, rs, dev):
        return functools.partial(
            pltpu.make_async_remote_copy,
            src_ref=src, dst_ref=dst, send_sem=ss, recv_sem=rs, device_id=dev, device_id_type=MESH,
        )

    def start(cond, *makes):
        @pl.when(cond)
        def _():
            for make in makes:
                if ending:
                    make().wait_send()
                else:
                    make().start()

    def incoming(dst, rs):
        return remote(dst, dst, loc.at[3], rs, (sib, c))

    def received(cond, *makes):
        if ending:
            return

        @pl.when(cond)
        def _():
            for make in makes:
                make().wait_recv()

    def pc(s, t):
        return p.at[s, pl.ds(t * NB, NB)]

    def ach(s, t):
        return ac.at[s, t]

    def a_rows(t):
        return a.at[pl.ds(t * NB, NB), pl.ds(0, NB)]

    def p_in(s, t):
        return incoming(pc(s, t), precv.at[s, t])

    def p_copy(s, t, src, z, way=0):
        return remote(src, pc(s, t), psend.at[s, t, way], precv.at[s, t], (r, z))

    def direct(s):
        return [
            remote(a_rows(0), pc(s, 0), zsend.at[i], precv.at[s, 0], (r, z))
            for i, z in enumerate([z for z in range(ncol - 1, -1, -1) if z != s])
        ]

    def spread(s, src):
        base = 0 if s == 0 else 1
        return [remote(src, k.at[s], ksib.at[s], krecv.at[s], (sib, c))] + [
            remote(src, k.at[s], ksend.at[s, j], krecv.at[s], (2 * j + base, c)) for j in range(chips - 1, 0, -1)
        ]

    def a_copies(t, src):
        over = remote(src, ach(core, t), asend.at[t, 0], arecv.at[core, t], (onward, c))
        across = remote(src, ach(core, t), asend.at[t, 1], arecv.at[core, t], (sib, c))
        return over, across

    def own(s):
        return pltpu.make_async_copy(a.at[:, pl.ds(0, NB)], p.at[s], loc.at[s])

    def own_slab():
        return [
            pltpu.make_async_copy(a.at[pl.ds(0, NB), pl.ds(t * CW, CW)], ach(core, t), slab.at[t]) for t in range(na)
        ]

    rest = range(1, nt)

    def p_source(here, ts):
        start(here & (c == 0), *[p_copy(0, t, pc(0, t), 1) for t in ts])
        start(
            here & (c == 1),
            *[p_copy(1, t, pc(1, t), z, i) for t in ts for i, z in enumerate((0, 2) if ncol > 2 else (0,))],
        )

    def opening():
        start((r == 0) & (c == 0), *direct(0))
        if not ending:
            for s in range(2):
                pl.when(c == s)(own(s).start)
        received((r == 0) & (c != 0), p_in(0, 0))
        if not ending:
            for s in range(2):
                pl.when(c == s)(own(s).wait)
        start((r == 1) & (c == 1), *direct(1))
        p_source(source & (c == 1), rest)
        start(r == 0, *spread(0, pc(0, 0)))
        p_source(q != 0, range(nt))
        received((q != 0) & first, incoming(k.at[0], krecv.at[0]))
        start((q != 0) & first, remote(k.at[0], k.at[0], ksib.at[0], krecv.at[0], (sib, c)))
        received(second, incoming(k.at[0], krecv.at[0]))
        if not ending:
            pl.when(source)(lambda: [copy.start() for copy in own_slab()] and None)

    def p_pass(t, s, z):
        here = (c == 1) if z == 1 else (c > 1) & (c < ncol - 1)
        if t == 0:
            here = here & (q != 0)
        received(here, p_in(s, t))
        start(here, p_copy(s, t, pc(s, t), c + 1))

    def direct_rest():
        start((r == 1) & (c == 0), *direct(0))

    def corner_rest():
        received((r == 1) & (c != 0), p_in(0, 0))
        received((r == 1) & (c != 1), p_in(1, 0))
        start(r == 1, *spread(1, pc(0, 0)), *spread(2, pc(1, 0)))

    def corner_pass():
        here = second & (q != 0)
        received(here, *[incoming(k.at[s], krecv.at[s]) for s in (1, 2)])
        start(here, *[remote(k.at[s], k.at[s], ksib.at[s], krecv.at[s], (sib, c)) for s in (1, 2)])

    def a_source():
        if not ending:
            pl.when(source)(lambda: [copy.wait() for copy in own_slab()] and None)
        makes = [a_copies(t, ach(core, t)) for t in range(na)]
        start(source, *[make for pair in makes for make in pair])

    def a_pass(t, at):
        here = pos == at if at < 3 else pos >= at
        over, across = a_copies(t, ach(core, t))
        received(here, incoming(ach(core, t), arecv.at[core, t]))
        if at < 3:
            start(here, over, across)
        else:
            start(here & (pos < chips - 1), over)
            start(here, across)

    half = NB // GROUP
    places = [[] for _ in range(4 * half)]

    def put(at, *step):
        places[min(int(at), 4 * half - 1)].append(functools.partial(*step))

    put(0, direct_rest)
    put(0, p_source, source & (c == 0), rest)
    put(0, a_source)
    put(2, corner_rest)
    put(5, corner_pass)
    for t in range(nt):
        if ncol > 2:
            put(1 + 2 * t, p_pass, t, 0, 1)
        if ncol > 3:
            put(2 + 2 * t, p_pass, t, 1, 2)
            put(5 + 3 * t, p_pass, t, 0, 2)
    for t in range(na):
        for at in range(1, min(chips, 4)):
            put(2 + 1.8 * t + 2.6 * (at - 1), a_pass, t, at)

    opening()

    eye = jnp.where(
        lax.broadcasted_iota(jnp.int32, (NB, NB), 0) == lax.broadcasted_iota(jnp.int32, (NB, NB), 1),
        f32(1.0), f32(0.0),
    )

    @pl.when(r == 0)
    def _():
        work[:, :NB] = p[0, :NB, :]

    @pl.when(r != 0)
    def _():
        work[:, :NB] = k[0]

    work[:, NB:] = eye

    def second_block():
        received(first, *[incoming(k.at[s], krecv.at[s]) for s in (1, 2)])

        @pl.when(r == 1)
        def _():
            k[1] = p[0, :NB, :]
            k[2] = p[1, :NB, :]

        l10 = dot(k[1], aug[0, :, NB:], 1, 1)
        low[...] = l10
        work[:, :NB] = k[2] - dot(l10, l10, 1, 1)
        work[:, NB:] = eye

    def group(g, carry):
        pl.when(g == half)(second_block)

        def visit(odd):
            for at, steps in enumerate(places):
                if steps and at % 2 == odd:
                    @pl.when(g == at // 2)
                    def _():
                        for step in steps:
                            step()

        u = eliminate(work, functools.partial(visit, 0))
        h = g // half
        top = lax.rem(g, half) * GROUP
        here = pl.ds(pl.multiple_of(top, GROUP), GROUP)
        aug[h, here, :NB] = pltpu.roll(u[:, :NB], top, 1)
        aug[h, here, NB:] = u[:, NB:]
        visit(1)
        return carry

    lax.fori_loop(0, 2 * half, group, 0)
    w0 = aug[0, :, NB:]
    l10 = low[...]

    w1 = aug[1, :, NB:]
    w10 = -dot(w1, dot(l10, w0))
    w = jnp.concatenate(
        [jnp.concatenate([w0, jnp.zeros((NB, NB), f32)], axis=1), jnp.concatenate([w10, w1], axis=1)], axis=0
    )
    wh, wl = two(w)
    w_left = jnp.concatenate([wh, wl, wh], axis=1)
    wh, wl = two(w.T)
    w_right = jnp.concatenate([wh, wh, wl], axis=0)

    def cols_part(t, carry):
        here = pl.ds(pl.multiple_of(t * CW, CW), CW)
        incoming(ac.at[1 - core, t], arecv.at[1 - core, t])().wait_recv()
        h0, l0 = two(ac[0, t])
        h1, l1 = two(ac[1, t])
        cols = mm(w_left, jnp.concatenate([h0, h1, h0, h1, l0, l1], axis=0))
        ch, cl = two(cols)
        right[:, here] = jnp.concatenate([ch, ch, cl], axis=0)
        return carry

    lax.fori_loop(0, na, cols_part, 0)

    @pl.when(r == 0)
    def _():
        p[1, :NB, :] = jnp.zeros((NB, NB), f32)

    def rows_part(t, carry):
        here = pl.ds(pl.multiple_of(t * NB, NB), NB)
        sent = (t > 0) | (q != 0)
        last = c == ncol - 1
        received(last & sent, p_in(0, t))
        received(((c == 0) | (last & (c > 1))) & sent, p_in(1, t))
        rh0, rl0 = two(p[0, here, :])
        rh1, rl1 = two(p[1, here, :])
        rows = mm(jnp.concatenate([rh0, rh1, rl0, rl1, rh0, rh1], axis=1), w_right)
        panel[here, :] = rows
        rh, rl = two(rows)
        left[here, :] = jnp.concatenate([rh, rl, rh], axis=1)
        return carry

    lax.fori_loop(0, nt, rows_part, 0)

    upper = lax.broadcasted_iota(jnp.int32, (NB, NB), 0) <= lax.broadcasted_iota(jnp.int32, (NB, NB), 1)

    @pl.when(r == 0)
    def _():
        panel[:NB, :NB] = jnp.where(upper, aug[0, :, :NB], f32(0.0)).T
        panel[:NB, NB:] = jnp.zeros((NB, NB), f32)

    @pl.when(r == 1)
    def _():
        panel[:NB, NB:] = jnp.where(upper, aug[1, :, :NB], f32(0.0)).T

    ending.append(True)
    opening()
    for steps in places:
        for step in steps:
            step()


def update_kernel(a, panel, left, right, out, held, sems):
    r = lax.axis_index("row")
    c = lax.axis_index("col")

    def copy(t):
        here = pl.ds(pl.multiple_of(t * TILE, TILE), TILE)
        return pltpu.make_async_copy(held.at[:, here], out.at[:, here], sems.at[t])

    def tile(t, carry):
        here = pl.ds(pl.multiple_of(t * TILE, TILE), TILE)
        held[:, here] = a[:, here] - mm(left[...], right[:, here])

        @pl.when(r < 2)
        def _():
            held[:NB, here] = jnp.zeros((NB, TILE), f32)

        for s in range(2):
            @pl.when((t == 0) & (c == s))
            def _():
                held[:, :NB] = panel[:, s * NB : (s + 1) * NB]

        copy(t).start()
        return carry

    tiles = a.shape[1] // TILE
    lax.fori_loop(0, tiles, tile, 0)
    for t in range(tiles):
        copy(t).wait()


def local(nrow, ncol, kernel):
    rows, cols = kernel.shape
    nt = rows // NB
    na = cols // CW
    chips = nrow // 2
    dma = pltpu.SemaphoreType.DMA
    panel, left, right = pl.pallas_call(
        functools.partial(panels_kernel, nrow, ncol, rows, cols),
        out_shape=[
            jax.ShapeDtypeStruct((rows, 2 * NB), f32),
            jax.ShapeDtypeStruct((rows, 6 * NB), bf16),
            jax.ShapeDtypeStruct((6 * NB, cols), bf16),
        ],
        in_specs=[pl.BlockSpec(memory_space=pltpu.HBM)],
        out_specs=[pl.BlockSpec(memory_space=pltpu.VMEM)] * 3,
        scratch_shapes=[
            pltpu.VMEM((2, rows, NB), f32),
            pltpu.VMEM((2, na, NB, CW), f32),
            pltpu.VMEM((3, NB, NB), f32),
            pltpu.VMEM((2, NB, 2 * NB), f32),
            pltpu.VMEM((NB, 2 * NB), f32),
            pltpu.VMEM((NB, NB), f32),
            dma((2, nt, 2)),
            dma((2, nt)),
            dma((ncol,)),
            dma((3, chips)),
            dma((3,)),
            dma((3,)),
            dma((na, 2)),
            dma((2, na)),
            dma((na,)),
            dma((4,)),
        ],
        compiler_params=pltpu.CompilerParams(
            collective_id=0, has_side_effects=True, vmem_limit_bytes=48 * 1024 * 1024
        ),
        name="panels",
    )(kernel)
    return pl.pallas_call(
        update_kernel,
        out_shape=jax.ShapeDtypeStruct((rows, cols), f32),
        in_specs=[pl.BlockSpec(memory_space=pltpu.VMEM)] * 4,
        out_specs=pl.BlockSpec(memory_space=pltpu.HBM),
        scratch_shapes=[pltpu.VMEM((rows, cols), f32), pltpu.SemaphoreType.DMA((cols // TILE,))],
        compiler_params=pltpu.CompilerParams(vmem_limit_bytes=32 * 1024 * 1024),
        name="update",
    )(kernel, panel, left, right)


def solution(mesh):
    return jax.shard_map(
        functools.partial(local, mesh.shape["row"], mesh.shape["col"]),
        mesh=mesh,
        in_specs=(P("row", "col"),),
        out_specs=P("row", "col"),
        check_vma=False,
    )
```

```python
import functools
import math

import jax
import jax.numpy as jnp
from jax import lax
from jax.experimental import pallas as pl
from jax.experimental.pallas import tpu as pltpu
from jax.sharding import PartitionSpec as P

NB = 128
SUB = 8
GROUP = 32
CW = 256
TILE = 256
MESH = pl.DeviceIdType.MESH
f32 = jnp.float32
bf16 = jnp.bfloat16


def dot(a, b, ca=1, cb=0):
    return lax.dot_general(
        a,
        b,
        (((ca,), (cb,)), ((), ())),
        precision=lax.Precision.HIGHEST,
        preferred_element_type=f32,
    )


def split(x):
    h = x.astype(bf16).astype(f32)
    rest = x - h
    m = rest.astype(bf16).astype(f32)
    return h, m, rest - m


def two(x):
    h = x.astype(bf16)
    return h, (x - h.astype(f32)).astype(bf16)


def mm(a, b):
    return jnp.dot(a, b, preferred_element_type=f32)


def splat(x, lane):
    return jnp.broadcast_to(x[:, lane : lane + 1], (SUB, NB))


def eliminate(work, midway):
    row = lax.broadcasted_iota(jnp.int32, (SUB, NB), 0)
    subs = GROUP // SUB
    rows = [
        [[jnp.broadcast_to(block[k : k + 1, h * NB : (h + 1) * NB], (SUB, NB)) for h in range(2)] for k in range(SUB)]
        for block in (work[s * SUB : (s + 1) * SUB, :] for s in range(subs))
    ]
    done = []
    for s in range(subs):
        mine = rows[s]
        wide = 2 * SUB if s + 1 < subs else SUB
        d = {(k, j): splat(mine[k][0], s * SUB + j) for k in range(SUB) for j in range(k, wide)}
        for j in range(SUB):
            inv = lax.rsqrt(d[j, j])
            for i in range(j + 1, wide):
                d[j, i] = d[j, i] * inv
            for i in range(j + 1, SUB):
                for l in range(i, wide):
                    d[i, l] = d[i, l] - d[j, i] * d[j, l]
            mine[j] = [x * inv for x in mine[j]]
            for i in range(j + 1, SUB):
                mine[i] = [x - d[j, i] * y for x, y in zip(mine[i], mine[j])]
        for later in range(s + 1, subs):
            for i in range(SUB):
                for k in range(SUB):
                    m = d[k, SUB + i] if later == s + 1 else splat(mine[k][0], later * SUB + i)
                    rows[later][i] = [x - m * y for x, y in zip(rows[later][i], mine[k])]
        halves = []
        for h in range(2):
            u = mine[0][h]
            for k in range(1, SUB):
                u = jnp.where(row == k, mine[k][h], u)
            halves.append(u)
        done.append(jnp.concatenate(halves, axis=1))
        if s == subs // 2 - 1:
            midway()
    u = jnp.concatenate(done, axis=0)
    h, m, l = split(u)
    left = jnp.concatenate([h, h, m, h, m, l], axis=0)[:, :NB].astype(bf16)
    right = jnp.concatenate([h, m, h, l, m, h], axis=0).astype(bf16)
    taken = lax.dot_general(left, right, (((0,), (0,)), ((), ())), preferred_element_type=f32)
    rest = work[GROUP:, :] - taken[GROUP:, :]
    work[: NB - GROUP, :NB] = pltpu.roll(rest[:, :NB], NB - GROUP, 1)
    work[: NB - GROUP, NB:] = rest[:, NB:]
    return u


def panels_kernel(
    nrow, ncol, rows_here, cols_here,
    a, panel, left, right,
    p, ac, k, aug, work, low,
    psend, precv, zsend, ksend, ksib, krecv, asend, arecv, slab, loc,
):
    chips = nrow // 2
    nx = math.isqrt(chips)
    ny = chips // nx
    nt = rows_here // NB
    na = cols_here // CW
    r = lax.axis_index("row")
    c = lax.axis_index("col")
    core = lax.rem(r, 2)
    q = r // 2
    qx = lax.rem(q, nx)
    qy = q // nx
    sib = r + 1 - 2 * core
    first = core == 0
    second = core == 1
    source = q == 0

    depth = qx + qy
    far_x = qx < nx - 1
    far_y = qy < ny - 1
    to_x = far_x & (first | (qy == 0))
    to_y = far_y & (second | (qx == 0))
    next_x = lax.rem(r + 2, nrow)
    next_y = lax.rem(r + 2 * nx, nrow)

    barrier = pltpu.get_barrier_semaphore()
    for i in range(1, ncol):
        pl.semaphore_signal(barrier, inc=1, device_id=(r, lax.rem(c + i, ncol)), device_id_type=MESH)
    for i in range(1, chips):
        pl.semaphore_signal(
            barrier, inc=1, device_id=(lax.rem(q + i, chips) * 2 + core, c), device_id_type=MESH
        )
    pl.semaphore_signal(barrier, inc=1, device_id=(sib, c), device_id_type=MESH)
    pl.semaphore_wait(barrier, ncol - 1 + chips)

    ending = []

    def remote(src, dst, ss, rs, dev):
        return functools.partial(
            pltpu.make_async_remote_copy,
            src_ref=src, dst_ref=dst, send_sem=ss, recv_sem=rs, device_id=dev, device_id_type=MESH,
        )

    def start(cond, *makes):
        @pl.when(cond)
        def _():
            for make in makes:
                if ending:
                    make().wait_send()
                else:
                    make().start()

    def incoming(dst, rs):
        return remote(dst, dst, loc.at[3], rs, (sib, c))

    def received(cond, *makes):
        if ending:
            return

        @pl.when(cond)
        def _():
            for make in makes:
                make().wait_recv()

    def pc(s, t):
        return p.at[s, pl.ds(t * NB, NB)]

    def ach(s, t):
        return ac.at[s, t]

    def a_rows(t):
        return a.at[pl.ds(t * NB, NB), pl.ds(0, NB)]

    def p_in(s, t):
        return incoming(pc(s, t), precv.at[s, t])

    def p_copy(s, t, src, z, way=0):
        return remote(src, pc(s, t), psend.at[s, t, way], precv.at[s, t], (r, z))

    def direct(s):
        return [
            remote(a_rows(0), pc(s, 0), zsend.at[i], precv.at[s, 0], (r, z))
            for i, z in enumerate([z for z in range(ncol - 1, -1, -1) if z != s])
        ]

    def spread(s, src):
        base = 0 if s == 0 else 1
        return [remote(src, k.at[s], ksib.at[s], krecv.at[s], (sib, c))] + [
            remote(src, k.at[s], ksend.at[s, j], krecv.at[s], (2 * j + base, c)) for j in range(chips - 1, 0, -1)
        ]

    def a_send(here, t):
        src = ach(core, t)

        def to(way, row):
            return remote(src, src, asend.at[t, way], arecv.at[core, t], (row, c))

        start(here & to_x, to(0, next_x))
        start(here & to_y, to(1, next_y))
        start(here, to(2, sib))

    def own(s):
        return pltpu.make_async_copy(a.at[:, pl.ds(0, NB)], p.at[s], loc.at[s])

    def own_slab():
        return [
            pltpu.make_async_copy(a.at[pl.ds(0, NB), pl.ds(t * CW, CW)], ach(core, t), slab.at[t]) for t in range(na)
        ]

    rest = range(1, nt)

    def p_source(here, ts):
        start(here & (c == 0), *[p_copy(0, t, pc(0, t), 1) for t in ts])
        start(
            here & (c == 1),
            *[p_copy(1, t, pc(1, t), z, i) for t in ts for i, z in enumerate((0, 2) if ncol > 2 else (0,))],
        )

    def opening():
        start((r == 0) & (c == 0), *direct(0))
        if not ending:
            for s in range(2):
                pl.when(c == s)(own(s).start)
        received((r == 0) & (c != 0), p_in(0, 0))
        if not ending:
            for s in range(2):
                pl.when(c == s)(own(s).wait)
        start((r == 1) & (c == 1), *direct(1))
        start(r == 0, *spread(0, pc(0, 0)))
        p_source((q != 0) & second, range(nt))
        received((q != 0) & first, incoming(k.at[0], krecv.at[0]))
        start((q != 0) & first, remote(k.at[0], k.at[0], ksib.at[0], krecv.at[0], (sib, c)))
        p_source((q != 0) & first, range(nt))
        p_source(source & (c == 1), rest)
        received(second, incoming(k.at[0], krecv.at[0]))
        if not ending:
            pl.when(source)(lambda: [copy.start() for copy in own_slab()] and None)

    def p_pass(t, s, z):
        here = (c == 1) if z == 1 else (c > 1) & (c < ncol - 1)
        if t == 0:
            here = here & (q != 0)
        received(here, p_in(s, t))
        start(here, p_copy(s, t, pc(s, t), c + 1))

    def direct_rest():
        start((r == 1) & (c == 0), *direct(0))

    def corner_rest():
        received((r == 1) & (c != 0), p_in(0, 0))
        received((r == 1) & (c != 1), p_in(1, 0))
        start(r == 1, *spread(1, pc(0, 0)), *spread(2, pc(1, 0)))

    def corner_pass():
        here = second & (q != 0)
        received(here, *[incoming(k.at[s], krecv.at[s]) for s in (1, 2)])
        start(here, *[remote(k.at[s], k.at[s], ksib.at[s], krecv.at[s], (sib, c)) for s in (1, 2)])

    def a_source():
        if not ending:
            pl.when(source)(lambda: [copy.wait() for copy in own_slab()] and None)
        for t in range(na):
            a_send(source, t)

    def a_pass(t, at):
        here = depth == at if at < 3 else depth >= at
        received(here, incoming(ach(core, t), arecv.at[core, t]))
        a_send(here, t)

    half = NB // GROUP
    places = [[] for _ in range(4 * half)]

    def put(at, *step):
        places[min(int(at), 4 * half - 1)].append(functools.partial(*step))

    put(0, direct_rest)
    put(0, p_source, source & (c == 0), rest)
    put(0, a_source)
    put(2, corner_rest)
    put(5, corner_pass)
    for t in range(nt):
        if ncol > 2:
            put(1 + 2 * t, p_pass, t, 0, 1)
        if ncol > 3:
            put(2 + 2 * t, p_pass, t, 1, 2)
            put(5 + 3 * t, p_pass, t, 0, 2)
    for t in range(na):
        for at in range(1, min(nx + ny - 1, 4)):
            put(2 * t + 2 * at, a_pass, t, at)

    opening()

    eye = jnp.where(
        lax.broadcasted_iota(jnp.int32, (NB, NB), 0) == lax.broadcasted_iota(jnp.int32, (NB, NB), 1),
        f32(1.0), f32(0.0),
    )

    @pl.when(r == 0)
    def _():
        work[:, :NB] = p[0, :NB, :]

    @pl.when(r != 0)
    def _():
        work[:, :NB] = k[0]

    work[:, NB:] = eye

    def second_block():
        received(first, *[incoming(k.at[s], krecv.at[s]) for s in (1, 2)])

        @pl.when(r == 1)
        def _():
            k[1] = p[0, :NB, :]
            k[2] = p[1, :NB, :]

        l10 = dot(k[1], aug[0, :, NB:], 1, 1)
        low[...] = l10
        work[:, :NB] = k[2] - dot(l10, l10, 1, 1)
        work[:, NB:] = eye

    def group(g, carry):
        pl.when(g == half)(second_block)

        def visit(odd):
            for at, steps in enumerate(places):
                if steps and at % 2 == odd:
                    @pl.when(g == at // 2)
                    def _():
                        for step in steps:
                            step()

        u = eliminate(work, functools.partial(visit, 0))
        h = g // half
        top = lax.rem(g, half) * GROUP
        here = pl.ds(pl.multiple_of(top, GROUP), GROUP)
        aug[h, here, :NB] = pltpu.roll(u[:, :NB], top, 1)
        aug[h, here, NB:] = u[:, NB:]
        visit(1)
        return carry

    lax.fori_loop(0, 2 * half, group, 0)
    w0 = aug[0, :, NB:]
    l10 = low[...]

    w1 = aug[1, :, NB:]
    w10 = -dot(w1, dot(l10, w0))
    w = jnp.concatenate(
        [jnp.concatenate([w0, jnp.zeros((NB, NB), f32)], axis=1), jnp.concatenate([w10, w1], axis=1)], axis=0
    )
    wh, wl = two(w)
    w_left = jnp.concatenate([wh, wl, wh], axis=1)
    wh, wl = two(w.T)
    w_right = jnp.concatenate([wh, wh, wl], axis=0)

    def cols_part(t, carry):
        here = pl.ds(pl.multiple_of(t * CW, CW), CW)
        incoming(ac.at[1 - core, t], arecv.at[1 - core, t])().wait_recv()
        h0, l0 = two(ac[0, t])
        h1, l1 = two(ac[1, t])
        cols = mm(w_left, jnp.concatenate([h0, h1, h0, h1, l0, l1], axis=0))
        ch, cl = two(cols)
        right[:, here] = jnp.concatenate([ch, ch, cl], axis=0)
        return carry

    lax.fori_loop(0, na, cols_part, 0)

    @pl.when(r == 0)
    def _():
        p[1, :NB, :] = jnp.zeros((NB, NB), f32)

    def rows_part(t, carry):
        here = pl.ds(pl.multiple_of(t * NB, NB), NB)
        sent = (t > 0) | (q != 0)
        last = c == ncol - 1
        received(last & sent, p_in(0, t))
        received(((c == 0) | (last & (c > 1))) & sent, p_in(1, t))
        rh0, rl0 = two(p[0, here, :])
        rh1, rl1 = two(p[1, here, :])
        rows = mm(jnp.concatenate([rh0, rh1, rl0, rl1, rh0, rh1], axis=1), w_right)
        panel[here, :] = rows
        rh, rl = two(rows)
        left[here, :] = jnp.concatenate([rh, rl, rh], axis=1)
        return carry

    lax.fori_loop(0, nt, rows_part, 0)

    upper = lax.broadcasted_iota(jnp.int32, (NB, NB), 0) <= lax.broadcasted_iota(jnp.int32, (NB, NB), 1)

    @pl.when(r == 0)
    def _():
        panel[:NB, :NB] = jnp.where(upper, aug[0, :, :NB], f32(0.0)).T
        panel[:NB, NB:] = jnp.zeros((NB, NB), f32)

    @pl.when(r == 1)
    def _():
        panel[:NB, NB:] = jnp.where(upper, aug[1, :, :NB], f32(0.0)).T

    ending.append(True)
    opening()
    for steps in places:
        for step in steps:
            step()


def update_kernel(a, panel, left, right, out, held, sems):
    r = lax.axis_index("row")
    c = lax.axis_index("col")

    def copy(t):
        here = pl.ds(pl.multiple_of(t * TILE, TILE), TILE)
        return pltpu.make_async_copy(held.at[:, here], out.at[:, here], sems.at[t])

    def tile(t, carry):
        here = pl.ds(pl.multiple_of(t * TILE, TILE), TILE)
        held[:, here] = a[:, here] - mm(left[...], right[:, here])

        @pl.when(r < 2)
        def _():
            held[:NB, here] = jnp.zeros((NB, TILE), f32)

        for s in range(2):
            @pl.when((t == 0) & (c == s))
            def _():
                held[:, :NB] = panel[:, s * NB : (s + 1) * NB]

        copy(t).start()
        return carry

    tiles = a.shape[1] // TILE
    lax.fori_loop(0, tiles, tile, 0)
    for t in range(tiles):
        copy(t).wait()


def local(nrow, ncol, kernel):
    rows, cols = kernel.shape
    nt = rows // NB
    na = cols // CW
    chips = nrow // 2
    dma = pltpu.SemaphoreType.DMA
    panel, left, right = pl.pallas_call(
        functools.partial(panels_kernel, nrow, ncol, rows, cols),
        out_shape=[
            jax.ShapeDtypeStruct((rows, 2 * NB), f32),
            jax.ShapeDtypeStruct((rows, 6 * NB), bf16),
            jax.ShapeDtypeStruct((6 * NB, cols), bf16),
        ],
        in_specs=[pl.BlockSpec(memory_space=pltpu.HBM)],
        out_specs=[pl.BlockSpec(memory_space=pltpu.VMEM)] * 3,
        scratch_shapes=[
            pltpu.VMEM((2, rows, NB), f32),
            pltpu.VMEM((2, na, NB, CW), f32),
            pltpu.VMEM((3, NB, NB), f32),
            pltpu.VMEM((2, NB, 2 * NB), f32),
            pltpu.VMEM((NB, 2 * NB), f32),
            pltpu.VMEM((NB, NB), f32),
            dma((2, nt, 2)),
            dma((2, nt)),
            dma((ncol,)),
            dma((3, chips)),
            dma((3,)),
            dma((3,)),
            dma((na, 3)),
            dma((2, na)),
            dma((na,)),
            dma((4,)),
        ],
        compiler_params=pltpu.CompilerParams(
            collective_id=0, has_side_effects=True, vmem_limit_bytes=48 * 1024 * 1024
        ),
        name="panels",
    )(kernel)
    return pl.pallas_call(
        update_kernel,
        out_shape=jax.ShapeDtypeStruct((rows, cols), f32),
        in_specs=[pl.BlockSpec(memory_space=pltpu.VMEM)] * 4,
        out_specs=pl.BlockSpec(memory_space=pltpu.HBM),
        scratch_shapes=[pltpu.VMEM((rows, cols), f32), pltpu.SemaphoreType.DMA((cols // TILE,))],
        compiler_params=pltpu.CompilerParams(vmem_limit_bytes=32 * 1024 * 1024),
        name="update",
    )(kernel, panel, left, right)


def solution(mesh):
    return jax.shard_map(
        functools.partial(local, mesh.shape["row"], mesh.shape["col"]),
        mesh=mesh,
        in_specs=(P("row", "col"),),
        out_specs=P("row", "col"),
        check_vma=False,
    )
```

```python
import functools
import math

import jax
import jax.numpy as jnp
from jax import lax
from jax.experimental import pallas as pl
from jax.experimental.pallas import tpu as pltpu
from jax.sharding import PartitionSpec as P

NB = 128
SUB = 8
GROUP = 32
CW = 128
TILE = 256
MESH = pl.DeviceIdType.MESH
f32 = jnp.float32
bf16 = jnp.bfloat16


def dot(a, b, ca=1, cb=0):
    return lax.dot_general(
        a,
        b,
        (((ca,), (cb,)), ((), ())),
        precision=lax.Precision.HIGHEST,
        preferred_element_type=f32,
    )


def split(x):
    h = x.astype(bf16).astype(f32)
    rest = x - h
    m = rest.astype(bf16).astype(f32)
    return h, m, rest - m


def two(x):
    h = x.astype(bf16)
    return h, (x - h.astype(f32)).astype(bf16)


def mm(a, b):
    return jnp.dot(a, b, preferred_element_type=f32)


def splat(x, lane):
    return jnp.broadcast_to(x[:, lane : lane + 1], (SUB, NB))


def eliminate(work, midway):
    row = lax.broadcasted_iota(jnp.int32, (SUB, NB), 0)
    subs = GROUP // SUB
    rows = [
        [[jnp.broadcast_to(block[k : k + 1, h * NB : (h + 1) * NB], (SUB, NB)) for h in range(2)] for k in range(SUB)]
        for block in (work[s * SUB : (s + 1) * SUB, :] for s in range(subs))
    ]
    done = []
    for s in range(subs):
        mine = rows[s]
        wide = 2 * SUB if s + 1 < subs else SUB
        d = {(k, j): splat(mine[k][0], s * SUB + j) for k in range(SUB) for j in range(k, wide)}
        for j in range(SUB):
            inv = lax.rsqrt(d[j, j])
            for i in range(j + 1, wide):
                d[j, i] = d[j, i] * inv
            for i in range(j + 1, SUB):
                for l in range(i, wide):
                    d[i, l] = d[i, l] - d[j, i] * d[j, l]
            mine[j] = [x * inv for x in mine[j]]
            for i in range(j + 1, SUB):
                mine[i] = [x - d[j, i] * y for x, y in zip(mine[i], mine[j])]
        for later in range(s + 1, subs):
            for i in range(SUB):
                for k in range(SUB):
                    m = d[k, SUB + i] if later == s + 1 else splat(mine[k][0], later * SUB + i)
                    rows[later][i] = [x - m * y for x, y in zip(rows[later][i], mine[k])]
        halves = []
        for h in range(2):
            u = mine[0][h]
            for k in range(1, SUB):
                u = jnp.where(row == k, mine[k][h], u)
            halves.append(u)
        done.append(jnp.concatenate(halves, axis=1))
        if s == subs // 2 - 1:
            midway()
    u = jnp.concatenate(done, axis=0)
    h, m, l = split(u)
    left = jnp.concatenate([h, h, m, h, m, l], axis=0)[:, :NB].astype(bf16)
    right = jnp.concatenate([h, m, h, l, m, h], axis=0).astype(bf16)
    taken = lax.dot_general(left, right, (((0,), (0,)), ((), ())), preferred_element_type=f32)
    rest = work[GROUP:, :] - taken[GROUP:, :]
    work[: NB - GROUP, :NB] = pltpu.roll(rest[:, :NB], NB - GROUP, 1)
    work[: NB - GROUP, NB:] = rest[:, NB:]
    return u


def panels_kernel(
    nrow, ncol, rows_here, cols_here,
    a, panel, left, right,
    p, ac, k, aug, work, low,
    psend, precv, zsend, ksend, ksib, krecv, asend, arecv, slab, loc,
):
    chips = nrow // 2
    nx = math.isqrt(chips)
    ny = chips // nx
    nt = rows_here // NB
    na = cols_here // CW
    r = lax.axis_index("row")
    c = lax.axis_index("col")
    core = lax.rem(r, 2)
    q = r // 2
    qx = lax.rem(q, nx)
    qy = q // nx
    sib = r + 1 - 2 * core
    first = core == 0
    second = core == 1
    source = q == 0

    oy = lax.rem(qy, 2)
    ox = lax.rem(qx, 2)
    if nx > 1 and ny > 1:
        pos_x = qy * nx + qx + oy * (nx - 1 - 2 * qx)
        pos_y = qx * ny + qy + ox * (ny - 1 - 2 * qy)
        step_x = jnp.where(oy == 0, jnp.where(qx < nx - 1, 1, nx), jnp.where(qx > 0, -1, nx))
        step_y = jnp.where(ox == 0, jnp.where(qy < ny - 1, nx, 1), jnp.where(qy > 0, -nx, 1))
        pos = jnp.where(first, pos_x, pos_y)
        onward = lax.rem(r + 2 * jnp.where(first, step_x, step_y) + nrow, nrow)
    else:
        pos = q
        onward = lax.rem(r + 2, nrow)

    barrier = pltpu.get_barrier_semaphore()
    for i in range(1, ncol):
        pl.semaphore_signal(barrier, inc=1, device_id=(r, lax.rem(c + i, ncol)), device_id_type=MESH)
    for i in range(1, chips):
        pl.semaphore_signal(
            barrier, inc=1, device_id=(lax.rem(q + i, chips) * 2 + core, c), device_id_type=MESH
        )
    pl.semaphore_signal(barrier, inc=1, device_id=(sib, c), device_id_type=MESH)
    pl.semaphore_wait(barrier, ncol - 1 + chips)

    ending = []

    def remote(src, dst, ss, rs, dev):
        return functools.partial(
            pltpu.make_async_remote_copy,
            src_ref=src, dst_ref=dst, send_sem=ss, recv_sem=rs, device_id=dev, device_id_type=MESH,
        )

    def start(cond, *makes):
        @pl.when(cond)
        def _():
            for make in makes:
                if ending:
                    make().wait_send()
                else:
                    make().start()

    def incoming(dst, rs):
        return remote(dst, dst, loc.at[3], rs, (sib, c))

    def received(cond, *makes):
        if ending:
            return

        @pl.when(cond)
        def _():
            for make in makes:
                make().wait_recv()

    def pc(s, t):
        return p.at[s, pl.ds(t * NB, NB)]

    def ach(s, t):
        return ac.at[s, t]

    def a_rows(t):
        return a.at[pl.ds(t * NB, NB), pl.ds(0, NB)]

    def p_in(s, t):
        return incoming(pc(s, t), precv.at[s, t])

    def p_copy(s, t, src, z, way=0):
        return remote(src, pc(s, t), psend.at[s, t, way], precv.at[s, t], (r, z))

    def direct(s):
        return [
            remote(a_rows(0), pc(s, 0), zsend.at[i], precv.at[s, 0], (r, z))
            for i, z in enumerate([z for z in range(ncol - 1, -1, -1) if z != s])
        ]

    def spread(s, src):
        base = 0 if s == 0 else 1
        return [remote(src, k.at[s], ksib.at[s], krecv.at[s], (sib, c))] + [
            remote(src, k.at[s], ksend.at[s, j], krecv.at[s], (2 * j + base, c)) for j in range(chips - 1, 0, -1)
        ]

    def a_copies(t, src):
        over = remote(src, ach(core, t), asend.at[t, 0], arecv.at[core, t], (onward, c))
        across = remote(src, ach(core, t), asend.at[t, 1], arecv.at[core, t], (sib, c))
        return over, across

    def own(s):
        return pltpu.make_async_copy(a.at[:, pl.ds(0, NB)], p.at[s], loc.at[s])

    def own_slab():
        return [
            pltpu.make_async_copy(a.at[pl.ds(0, NB), pl.ds(t * CW, CW)], ach(core, t), slab.at[t]) for t in range(na)
        ]

    rest = range(1, nt)

    def p_source(here, ts):
        start(here & (c == 0), *[p_copy(0, t, pc(0, t), 1) for t in ts])
        start(
            here & (c == 1),
            *[p_copy(1, t, pc(1, t), z, i) for t in ts for i, z in enumerate((0, 2) if ncol > 2 else (0,))],
        )

    def opening():
        start((r == 0) & (c == 0), *direct(0))
        if not ending:
            for s in range(2):
                pl.when(c == s)(own(s).start)
        received((r == 0) & (c != 0), p_in(0, 0))
        if not ending:
            for s in range(2):
                pl.when(c == s)(own(s).wait)
        start((r == 1) & (c == 1), *direct(1))
        start(r == 0, *spread(0, pc(0, 0)))
        p_source((q != 0) & second, range(nt))
        received((q != 0) & first, incoming(k.at[0], krecv.at[0]))
        start((q != 0) & first, remote(k.at[0], k.at[0], ksib.at[0], krecv.at[0], (sib, c)))
        p_source((q != 0) & first, range(nt))
        p_source(source & (c == 1), rest)
        received(second, incoming(k.at[0], krecv.at[0]))
        if not ending:
            pl.when(source)(lambda: [copy.start() for copy in own_slab()] and None)

    def p_pass(t, s, z):
        here = (c == 1) if z == 1 else (c > 1) & (c < ncol - 1)
        if t == 0:
            here = here & (q != 0)
        received(here, p_in(s, t))
        start(here, p_copy(s, t, pc(s, t), c + 1))

    def direct_rest():
        start((r == 1) & (c == 0), *direct(0))

    def corner_rest():
        received((r == 1) & (c != 0), p_in(0, 0))
        received((r == 1) & (c != 1), p_in(1, 0))
        start(r == 1, *spread(1, pc(0, 0)), *spread(2, pc(1, 0)))

    def corner_pass():
        here = second & (q != 0)
        received(here, *[incoming(k.at[s], krecv.at[s]) for s in (1, 2)])
        start(here, *[remote(k.at[s], k.at[s], ksib.at[s], krecv.at[s], (sib, c)) for s in (1, 2)])

    def a_source():
        if not ending:
            pl.when(source)(lambda: [copy.wait() for copy in own_slab()] and None)
        makes = [a_copies(t, ach(core, t)) for t in range(na)]
        start(source, *[make for pair in makes for make in pair])

    def a_pass(t, at):
        here = pos == at if at < 3 else pos >= at
        over, across = a_copies(t, ach(core, t))
        received(here, incoming(ach(core, t), arecv.at[core, t]))
        if at < 3:
            start(here, over, across)
        else:
            start(here & (pos < chips - 1), over)
            start(here, across)

    half = NB // GROUP
    places = [[] for _ in range(4 * half)]

    def put(at, *step):
        places[min(int(at), 4 * half - 1)].append(functools.partial(*step))

    put(0, direct_rest)
    put(0, p_source, source & (c == 0), rest)
    put(0, a_source)
    put(2, corner_rest)
    put(5, corner_pass)
    for t in range(nt):
        if ncol > 2:
            put(1 + 2 * t, p_pass, t, 0, 1)
        if ncol > 3:
            put(2 + 2 * t, p_pass, t, 1, 2)
            put(5 + 3 * t, p_pass, t, 0, 2)
    for t in range(na):
        for at in range(1, min(chips, 4)):
            put(1.5 + 0.9 * t + 1.8 * (at - 1), a_pass, t, at)

    opening()

    eye = jnp.where(
        lax.broadcasted_iota(jnp.int32, (NB, NB), 0) == lax.broadcasted_iota(jnp.int32, (NB, NB), 1),
        f32(1.0), f32(0.0),
    )

    @pl.when(r == 0)
    def _():
        work[:, :NB] = p[0, :NB, :]

    @pl.when(r != 0)
    def _():
        work[:, :NB] = k[0]

    work[:, NB:] = eye

    def second_block():
        received(first, *[incoming(k.at[s], krecv.at[s]) for s in (1, 2)])

        @pl.when(r == 1)
        def _():
            k[1] = p[0, :NB, :]
            k[2] = p[1, :NB, :]

        l10 = dot(k[1], aug[0, :, NB:], 1, 1)
        low[...] = l10
        work[:, :NB] = k[2] - dot(l10, l10, 1, 1)
        work[:, NB:] = eye

    def group(g, carry):
        pl.when(g == half)(second_block)

        def visit(odd):
            for at, steps in enumerate(places):
                if steps and at % 2 == odd:
                    @pl.when(g == at // 2)
                    def _():
                        for step in steps:
                            step()

        u = eliminate(work, functools.partial(visit, 0))
        h = g // half
        top = lax.rem(g, half) * GROUP
        here = pl.ds(pl.multiple_of(top, GROUP), GROUP)
        aug[h, here, :NB] = pltpu.roll(u[:, :NB], top, 1)
        aug[h, here, NB:] = u[:, NB:]
        visit(1)
        return carry

    lax.fori_loop(0, 2 * half, group, 0)
    w0 = aug[0, :, NB:]
    l10 = low[...]

    w1 = aug[1, :, NB:]
    w10 = -dot(w1, dot(l10, w0))
    w = jnp.concatenate(
        [jnp.concatenate([w0, jnp.zeros((NB, NB), f32)], axis=1), jnp.concatenate([w10, w1], axis=1)], axis=0
    )
    wh, wl = two(w)
    w_left = jnp.concatenate([wh, wl, wh], axis=1)
    wh, wl = two(w.T)
    w_right = jnp.concatenate([wh, wh, wl], axis=0)

    def cols_part(t, carry):
        here = pl.ds(pl.multiple_of(t * CW, CW), CW)
        incoming(ac.at[1 - core, t], arecv.at[1 - core, t])().wait_recv()
        h0, l0 = two(ac[0, t])
        h1, l1 = two(ac[1, t])
        cols = mm(w_left, jnp.concatenate([h0, h1, h0, h1, l0, l1], axis=0))
        ch, cl = two(cols)
        right[:, here] = jnp.concatenate([ch, ch, cl], axis=0)
        return carry

    lax.fori_loop(0, na, cols_part, 0)

    @pl.when(r == 0)
    def _():
        p[1, :NB, :] = jnp.zeros((NB, NB), f32)

    def rows_part(t, carry):
        here = pl.ds(pl.multiple_of(t * NB, NB), NB)
        sent = (t > 0) | (q != 0)
        last = c == ncol - 1
        received(last & sent, p_in(0, t))
        received(((c == 0) | (last & (c > 1))) & sent, p_in(1, t))
        rh0, rl0 = two(p[0, here, :])
        rh1, rl1 = two(p[1, here, :])
        rows = mm(jnp.concatenate([rh0, rh1, rl0, rl1, rh0, rh1], axis=1), w_right)
        panel[here, :] = rows
        rh, rl = two(rows)
        left[here, :] = jnp.concatenate([rh, rl, rh], axis=1)
        return carry

    lax.fori_loop(0, nt, rows_part, 0)

    upper = lax.broadcasted_iota(jnp.int32, (NB, NB), 0) <= lax.broadcasted_iota(jnp.int32, (NB, NB), 1)

    @pl.when(r == 0)
    def _():
        panel[:NB, :NB] = jnp.where(upper, aug[0, :, :NB], f32(0.0)).T
        panel[:NB, NB:] = jnp.zeros((NB, NB), f32)

    @pl.when(r == 1)
    def _():
        panel[:NB, NB:] = jnp.where(upper, aug[1, :, :NB], f32(0.0)).T

    ending.append(True)
    opening()
    for steps in places:
        for step in steps:
            step()


def update_kernel(a, panel, left, right, out, held, sems):
    r = lax.axis_index("row")
    c = lax.axis_index("col")

    def copy(t):
        here = pl.ds(pl.multiple_of(t * TILE, TILE), TILE)
        return pltpu.make_async_copy(held.at[:, here], out.at[:, here], sems.at[t])

    def tile(t, carry):
        here = pl.ds(pl.multiple_of(t * TILE, TILE), TILE)
        held[:, here] = a[:, here] - mm(left[...], right[:, here])

        @pl.when(r < 2)
        def _():
            held[:NB, here] = jnp.zeros((NB, TILE), f32)

        for s in range(2):
            @pl.when((t == 0) & (c == s))
            def _():
                held[:, :NB] = panel[:, s * NB : (s + 1) * NB]

        copy(t).start()
        return carry

    tiles = a.shape[1] // TILE
    lax.fori_loop(0, tiles, tile, 0)
    for t in range(tiles):
        copy(t).wait()


def local(nrow, ncol, kernel):
    rows, cols = kernel.shape
    nt = rows // NB
    na = cols // CW
    chips = nrow // 2
    dma = pltpu.SemaphoreType.DMA
    panel, left, right = pl.pallas_call(
        functools.partial(panels_kernel, nrow, ncol, rows, cols),
        out_shape=[
            jax.ShapeDtypeStruct((rows, 2 * NB), f32),
            jax.ShapeDtypeStruct((rows, 6 * NB), bf16),
            jax.ShapeDtypeStruct((6 * NB, cols), bf16),
        ],
        in_specs=[pl.BlockSpec(memory_space=pltpu.HBM)],
        out_specs=[pl.BlockSpec(memory_space=pltpu.VMEM)] * 3,
        scratch_shapes=[
            pltpu.VMEM((2, rows, NB), f32),
            pltpu.VMEM((2, na, NB, CW), f32),
            pltpu.VMEM((3, NB, NB), f32),
            pltpu.VMEM((2, NB, 2 * NB), f32),
            pltpu.VMEM((NB, 2 * NB), f32),
            pltpu.VMEM((NB, NB), f32),
            dma((2, nt, 2)),
            dma((2, nt)),
            dma((ncol,)),
            dma((3, chips)),
            dma((3,)),
            dma((3,)),
            dma((na, 2)),
            dma((2, na)),
            dma((na,)),
            dma((4,)),
        ],
        compiler_params=pltpu.CompilerParams(
            collective_id=0, has_side_effects=True, vmem_limit_bytes=48 * 1024 * 1024
        ),
        name="panels",
    )(kernel)
    return pl.pallas_call(
        update_kernel,
        out_shape=jax.ShapeDtypeStruct((rows, cols), f32),
        in_specs=[pl.BlockSpec(memory_space=pltpu.VMEM)] * 4,
        out_specs=pl.BlockSpec(memory_space=pltpu.HBM),
        scratch_shapes=[pltpu.VMEM((rows, cols), f32), pltpu.SemaphoreType.DMA((cols // TILE,))],
        compiler_params=pltpu.CompilerParams(vmem_limit_bytes=32 * 1024 * 1024),
        name="update",
    )(kernel, panel, left, right)


def solution(mesh):
    return jax.shard_map(
        functools.partial(local, mesh.shape["row"], mesh.shape["col"]),
        mesh=mesh,
        in_specs=(P("row", "col"),),
        out_specs=P("row", "col"),
        check_vma=False,
    )
```

```python
import functools
import math

import jax
import jax.numpy as jnp
from jax import lax
from jax.experimental import pallas as pl
from jax.experimental.pallas import tpu as pltpu
from jax.sharding import PartitionSpec as P

NB = 128
SUB = 8
GROUP = 32
CW = 256
TILE = 256
MESH = pl.DeviceIdType.MESH
f32 = jnp.float32
bf16 = jnp.bfloat16


def dot(a, b, ca=1, cb=0):
    return lax.dot_general(
        a,
        b,
        (((ca,), (cb,)), ((), ())),
        precision=lax.Precision.HIGHEST,
        preferred_element_type=f32,
    )


def split(x):
    h = x.astype(bf16).astype(f32)
    rest = x - h
    m = rest.astype(bf16).astype(f32)
    return h, m, rest - m


def two(x):
    h = x.astype(bf16)
    return h, (x - h.astype(f32)).astype(bf16)


def mm(a, b):
    return jnp.dot(a, b, preferred_element_type=f32)


def splat(x, lane):
    return jnp.broadcast_to(x[:, lane : lane + 1], (SUB, NB))


def eliminate(work, midway):
    row = lax.broadcasted_iota(jnp.int32, (SUB, NB), 0)
    subs = GROUP // SUB
    rows = [
        [[jnp.broadcast_to(block[k : k + 1, h * NB : (h + 1) * NB], (SUB, NB)) for h in range(2)] for k in range(SUB)]
        for block in (work[s * SUB : (s + 1) * SUB, :] for s in range(subs))
    ]
    done = []
    for s in range(subs):
        mine = rows[s]
        wide = 2 * SUB if s + 1 < subs else SUB
        d = {(k, j): splat(mine[k][0], s * SUB + j) for k in range(SUB) for j in range(k, wide)}
        for j in range(SUB):
            inv = lax.rsqrt(d[j, j])
            for i in range(j + 1, wide):
                d[j, i] = d[j, i] * inv
            for i in range(j + 1, SUB):
                for l in range(i, wide):
                    d[i, l] = d[i, l] - d[j, i] * d[j, l]
            mine[j] = [x * inv for x in mine[j]]
            for i in range(j + 1, SUB):
                mine[i] = [x - d[j, i] * y for x, y in zip(mine[i], mine[j])]
        for later in range(s + 1, subs):
            for i in range(SUB):
                for k in range(SUB):
                    m = d[k, SUB + i] if later == s + 1 else splat(mine[k][0], later * SUB + i)
                    rows[later][i] = [x - m * y for x, y in zip(rows[later][i], mine[k])]
        halves = []
        for h in range(2):
            u = mine[0][h]
            for k in range(1, SUB):
                u = jnp.where(row == k, mine[k][h], u)
            halves.append(u)
        done.append(jnp.concatenate(halves, axis=1))
        if s == subs // 2 - 1:
            midway()
    u = jnp.concatenate(done, axis=0)
    h, m, l = split(u)
    left = jnp.concatenate([h, h, m, h, m, l], axis=0)[:, :NB].astype(bf16)
    right = jnp.concatenate([h, m, h, l, m, h], axis=0).astype(bf16)
    taken = lax.dot_general(left, right, (((0,), (0,)), ((), ())), preferred_element_type=f32)
    rest = work[GROUP:, :] - taken[GROUP:, :]
    work[: NB - GROUP, :NB] = pltpu.roll(rest[:, :NB], NB - GROUP, 1)
    work[: NB - GROUP, NB:] = rest[:, NB:]
    return u


def panels_kernel(
    nrow, ncol, rows_here, cols_here,
    a, panel, left, right,
    p, ac, k, aug, work, low,
    psend, precv, zsend, ksend, ksib, krecv, asend, arecv, slab, loc,
):
    chips = nrow // 2
    nx = math.isqrt(chips)
    ny = chips // nx
    nt = rows_here // NB
    na = cols_here // CW
    r = lax.axis_index("row")
    c = lax.axis_index("col")
    core = lax.rem(r, 2)
    q = r // 2
    qx = lax.rem(q, nx)
    qy = q // nx
    sib = r + 1 - 2 * core
    first = core == 0
    second = core == 1
    source = q == 0

    oy = lax.rem(qy, 2)
    ox = lax.rem(qx, 2)
    if nx > 1 and ny > 1:
        pos_x = qy * nx + qx + oy * (nx - 1 - 2 * qx)
        pos_y = qx * ny + qy + ox * (ny - 1 - 2 * qy)
        step_x = jnp.where(oy == 0, jnp.where(qx < nx - 1, 1, nx), jnp.where(qx > 0, -1, nx))
        step_y = jnp.where(ox == 0, jnp.where(qy < ny - 1, nx, 1), jnp.where(qy > 0, -nx, 1))
        pos = jnp.where(first, pos_x, pos_y)
        onward = lax.rem(r + 2 * jnp.where(first, step_x, step_y) + nrow, nrow)
    else:
        pos = q
        onward = lax.rem(r + 2, nrow)

    barrier = pltpu.get_barrier_semaphore()
    for i in range(1, ncol):
        pl.semaphore_signal(barrier, inc=1, device_id=(r, lax.rem(c + i, ncol)), device_id_type=MESH)
    for i in range(1, chips):
        pl.semaphore_signal(
            barrier, inc=1, device_id=(lax.rem(q + i, chips) * 2 + core, c), device_id_type=MESH
        )
    pl.semaphore_signal(barrier, inc=1, device_id=(sib, c), device_id_type=MESH)
    pl.semaphore_wait(barrier, ncol - 1 + chips)

    ending = []

    def remote(src, dst, ss, rs, dev):
        return functools.partial(
            pltpu.make_async_remote_copy,
            src_ref=src, dst_ref=dst, send_sem=ss, recv_sem=rs, device_id=dev, device_id_type=MESH,
        )

    def start(cond, *makes):
        @pl.when(cond)
        def _():
            for make in makes:
                if ending:
                    make().wait_send()
                else:
                    make().start()

    def incoming(dst, rs):
        return remote(dst, dst, loc.at[3], rs, (sib, c))

    def received(cond, *makes):
        if ending:
            return

        @pl.when(cond)
        def _():
            for make in makes:
                make().wait_recv()

    def pc(s, t):
        return p.at[s, pl.ds(t * NB, NB)]

    def ach(s, t):
        return ac.at[s, t]

    def a_rows(t):
        return a.at[pl.ds(t * NB, NB), pl.ds(0, NB)]

    def p_in(s, t):
        return incoming(pc(s, t), precv.at[s, t])

    def p_copy(s, t, src, z, way=0):
        return remote(src, pc(s, t), psend.at[s, t, way], precv.at[s, t], (r, z))

    def direct(s):
        return [
            remote(a_rows(0), pc(s, 0), zsend.at[i], precv.at[s, 0], (r, z))
            for i, z in enumerate([z for z in range(ncol - 1, -1, -1) if z != s])
        ]

    def spread(s, src):
        base = 0 if s == 0 else 1
        return [remote(src, k.at[s], ksib.at[s], krecv.at[s], (sib, c))] + [
            remote(src, k.at[s], ksend.at[s, j], krecv.at[s], (2 * j + base, c)) for j in range(chips - 1, 0, -1)
        ]

    def a_copies(t, src):
        over = remote(src, ach(core, t), asend.at[t, 0], arecv.at[core, t], (onward, c))
        across = remote(src, ach(core, t), asend.at[t, 1], arecv.at[core, t], (sib, c))
        return over, across

    def own(s):
        return pltpu.make_async_copy(a.at[:, pl.ds(0, NB)], p.at[s], loc.at[s])

    def own_slab():
        return [
            pltpu.make_async_copy(a.at[pl.ds(0, NB), pl.ds(t * CW, CW)], ach(core, t), slab.at[t]) for t in range(na)
        ]

    rest = range(1, nt)

    def p_source(here, ts):
        start(here & (c == 0), *[p_copy(0, t, pc(0, t), 1) for t in ts])
        start(
            here & (c == 1),
            *[p_copy(1, t, pc(1, t), z, i) for t in ts for i, z in enumerate((0, 2) if ncol > 2 else (0,))],
        )

    def opening():
        start((r == 0) & (c == 0), *direct(0))
        if not ending:
            for s in range(2):
                pl.when(c == s)(own(s).start)
        received((r == 0) & (c != 0), p_in(0, 0))
        if not ending:
            for s in range(2):
                pl.when(c == s)(own(s).wait)
        start((r == 1) & (c == 1), *direct(1))
        start(r == 0, *spread(0, pc(0, 0)))
        p_source((q != 0) & second, range(nt))
        received((q != 0) & first, incoming(k.at[0], krecv.at[0]))
        start((q != 0) & first, remote(k.at[0], k.at[0], ksib.at[0], krecv.at[0], (sib, c)))
        p_source((q != 0) & first, range(nt))
        p_source(source & (c == 1), rest)
        received(second, incoming(k.at[0], krecv.at[0]))
        if not ending:
            pl.when(source)(lambda: [copy.start() for copy in own_slab()] and None)

    def p_pass(t, s, z):
        here = (c == 1) if z == 1 else (c > 1) & (c < ncol - 1)
        if t == 0:
            here = here & (q != 0)
        received(here, p_in(s, t))
        start(here, p_copy(s, t, pc(s, t), c + 1))

    def direct_rest():
        start((r == 1) & (c == 0), *direct(0))

    def corner_rest():
        received((r == 1) & (c != 0), p_in(0, 0))
        received((r == 1) & (c != 1), p_in(1, 0))
        start(r == 1, *spread(1, pc(0, 0)), *spread(2, pc(1, 0)))

    def corner_pass():
        here = second & (q != 0)
        received(here, *[incoming(k.at[s], krecv.at[s]) for s in (1, 2)])
        start(here, *[remote(k.at[s], k.at[s], ksib.at[s], krecv.at[s], (sib, c)) for s in (1, 2)])

    def a_source():
        if not ending:
            pl.when(source)(lambda: [copy.wait() for copy in own_slab()] and None)
        makes = [a_copies(t, ach(core, t)) for t in range(na)]
        start(source, *[make for pair in makes for make in pair])

    def a_pass(t, at):
        here = pos == at if at < 3 else pos >= at
        over, across = a_copies(t, ach(core, t))
        received(here, incoming(ach(core, t), arecv.at[core, t]))
        if at < 3:
            start(here, over, across)
        else:
            start(here & (pos < chips - 1), over)
            start(here, across)

    half = NB // GROUP
    places = [[] for _ in range(4 * half)]

    def put(at, *step):
        places[min(int(at), 4 * half - 1)].append(functools.partial(*step))

    put(2, corner_rest)
    put(5, corner_pass)
    for t in range(nt):
        if ncol > 2:
            put(1 + 2 * t, p_pass, t, 0, 1)
        if ncol > 3:
            put(2 + 2 * t, p_pass, t, 1, 2)
            put(5 + 3 * t, p_pass, t, 0, 2)
    for t in range(na):
        for at in range(1, min(chips, 4)):
            put(2 + 1.8 * t + 2.6 * (at - 1), a_pass, t, at)

    def begin():
        opening()
        direct_rest()
        a_source()
        p_source(source & (c == 0), rest)

    begin()

    eye = jnp.where(
        lax.broadcasted_iota(jnp.int32, (NB, NB), 0) == lax.broadcasted_iota(jnp.int32, (NB, NB), 1),
        f32(1.0), f32(0.0),
    )

    @pl.when(r == 0)
    def _():
        work[:, :NB] = p[0, :NB, :]

    @pl.when(r != 0)
    def _():
        work[:, :NB] = k[0]

    work[:, NB:] = eye

    def second_block():
        received(first, *[incoming(k.at[s], krecv.at[s]) for s in (1, 2)])

        @pl.when(r == 1)
        def _():
            k[1] = p[0, :NB, :]
            k[2] = p[1, :NB, :]

        l10 = dot(k[1], aug[0, :, NB:], 1, 1)
        low[...] = l10
        work[:, :NB] = k[2] - dot(l10, l10, 1, 1)
        work[:, NB:] = eye

    def group(g, carry):
        pl.when(g == half)(second_block)

        def visit(odd):
            for at, steps in enumerate(places):
                if steps and at % 2 == odd:
                    @pl.when(g == at // 2)
                    def _():
                        for step in steps:
                            step()

        u = eliminate(work, functools.partial(visit, 0))
        h = g // half
        top = lax.rem(g, half) * GROUP
        here = pl.ds(pl.multiple_of(top, GROUP), GROUP)
        aug[h, here, :NB] = pltpu.roll(u[:, :NB], top, 1)
        aug[h, here, NB:] = u[:, NB:]
        visit(1)
        return carry

    lax.fori_loop(0, 2 * half, group, 0)
    w0 = aug[0, :, NB:]
    l10 = low[...]

    w1 = aug[1, :, NB:]
    w10 = -dot(w1, dot(l10, w0))
    w = jnp.concatenate(
        [jnp.concatenate([w0, jnp.zeros((NB, NB), f32)], axis=1), jnp.concatenate([w10, w1], axis=1)], axis=0
    )
    wh, wl = two(w)
    w_left = jnp.concatenate([wh, wl, wh], axis=1)
    wh, wl = two(w.T)
    w_right = jnp.concatenate([wh, wh, wl], axis=0)

    def cols_part(t, carry):
        here = pl.ds(pl.multiple_of(t * CW, CW), CW)
        incoming(ac.at[1 - core, t], arecv.at[1 - core, t])().wait_recv()
        h0, l0 = two(ac[0, t])
        h1, l1 = two(ac[1, t])
        cols = mm(w_left, jnp.concatenate([h0, h1, h0, h1, l0, l1], axis=0))
        ch, cl = two(cols)
        right[:, here] = jnp.concatenate([ch, ch, cl], axis=0)
        return carry

    lax.fori_loop(0, na, cols_part, 0)

    @pl.when(r == 0)
    def _():
        p[1, :NB, :] = jnp.zeros((NB, NB), f32)

    def rows_part(t, carry):
        here = pl.ds(pl.multiple_of(t * NB, NB), NB)
        sent = (t > 0) | (q != 0)
        last = c == ncol - 1
        received(last & sent, p_in(0, t))
        received(((c == 0) | (last & (c > 1))) & sent, p_in(1, t))
        rh0, rl0 = two(p[0, here, :])
        rh1, rl1 = two(p[1, here, :])
        rows = mm(jnp.concatenate([rh0, rh1, rl0, rl1, rh0, rh1], axis=1), w_right)
        panel[here, :] = rows
        rh, rl = two(rows)
        left[here, :] = jnp.concatenate([rh, rl, rh], axis=1)
        return carry

    lax.fori_loop(0, nt, rows_part, 0)

    upper = lax.broadcasted_iota(jnp.int32, (NB, NB), 0) <= lax.broadcasted_iota(jnp.int32, (NB, NB), 1)

    @pl.when(r == 0)
    def _():
        panel[:NB, :NB] = jnp.where(upper, aug[0, :, :NB], f32(0.0)).T
        panel[:NB, NB:] = jnp.zeros((NB, NB), f32)

    @pl.when(r == 1)
    def _():
        panel[:NB, NB:] = jnp.where(upper, aug[1, :, :NB], f32(0.0)).T

    ending.append(True)
    begin()
    for steps in places:
        for step in steps:
            step()


def update_kernel(a, panel, left, right, out, held, sems):
    r = lax.axis_index("row")
    c = lax.axis_index("col")

    def copy(t):
        here = pl.ds(pl.multiple_of(t * TILE, TILE), TILE)
        return pltpu.make_async_copy(held.at[:, here], out.at[:, here], sems.at[t])

    def tile(t, carry):
        here = pl.ds(pl.multiple_of(t * TILE, TILE), TILE)
        held[:, here] = a[:, here] - mm(left[...], right[:, here])

        @pl.when(r < 2)
        def _():
            held[:NB, here] = jnp.zeros((NB, TILE), f32)

        for s in range(2):
            @pl.when((t == 0) & (c == s))
            def _():
                held[:, :NB] = panel[:, s * NB : (s + 1) * NB]

        copy(t).start()
        return carry

    tiles = a.shape[1] // TILE
    lax.fori_loop(0, tiles, tile, 0)
    for t in range(tiles):
        copy(t).wait()


def local(nrow, ncol, kernel):
    rows, cols = kernel.shape
    nt = rows // NB
    na = cols // CW
    chips = nrow // 2
    dma = pltpu.SemaphoreType.DMA
    panel, left, right = pl.pallas_call(
        functools.partial(panels_kernel, nrow, ncol, rows, cols),
        out_shape=[
            jax.ShapeDtypeStruct((rows, 2 * NB), f32),
            jax.ShapeDtypeStruct((rows, 6 * NB), bf16),
            jax.ShapeDtypeStruct((6 * NB, cols), bf16),
        ],
        in_specs=[pl.BlockSpec(memory_space=pltpu.HBM)],
        out_specs=[pl.BlockSpec(memory_space=pltpu.VMEM)] * 3,
        scratch_shapes=[
            pltpu.VMEM((2, rows, NB), f32),
            pltpu.VMEM((2, na, NB, CW), f32),
            pltpu.VMEM((3, NB, NB), f32),
            pltpu.VMEM((2, NB, 2 * NB), f32),
            pltpu.VMEM((NB, 2 * NB), f32),
            pltpu.VMEM((NB, NB), f32),
            dma((2, nt, 2)),
            dma((2, nt)),
            dma((ncol,)),
            dma((3, chips)),
            dma((3,)),
            dma((3,)),
            dma((na, 2)),
            dma((2, na)),
            dma((na,)),
            dma((4,)),
        ],
        compiler_params=pltpu.CompilerParams(
            collective_id=0, has_side_effects=True, vmem_limit_bytes=48 * 1024 * 1024
        ),
        name="panels",
    )(kernel)
    return pl.pallas_call(
        update_kernel,
        out_shape=jax.ShapeDtypeStruct((rows, cols), f32),
        in_specs=[pl.BlockSpec(memory_space=pltpu.VMEM)] * 4,
        out_specs=pl.BlockSpec(memory_space=pltpu.HBM),
        scratch_shapes=[pltpu.VMEM((rows, cols), f32), pltpu.SemaphoreType.DMA((cols // TILE,))],
        compiler_params=pltpu.CompilerParams(vmem_limit_bytes=32 * 1024 * 1024),
        name="update",
    )(kernel, panel, left, right)


def solution(mesh):
    return jax.shard_map(
        functools.partial(local, mesh.shape["row"], mesh.shape["col"]),
        mesh=mesh,
        in_specs=(P("row", "col"),),
        out_specs=P("row", "col"),
        check_vma=False,
    )
```
